512 devices in a mesh: dp: 64 (over z_lo, y, x), mp: 8 (over z_hi, core).
Axes of the slice: x: 4, y: 4, z: 16 (z_hi: 4, z_lo: 4; z = z_hi * 4 + z_lo), core: 2. Of those that a mesh axis runs over, the one named last changes fastest.
Arguments:
- grads: bfloat16 [64, 16, 512, 512], P('dp', 'mp')
- prev_roots: bfloat16 [16, 2, 512, 512], P('mp')
- damping: float32 [4], replicated, may hold values from 0.05 to 1
- block_layer: int32 [16], P('mp'), may hold values from 0 to 3
- owners: int32 [16, 2], P('mp'), may hold values from -1 to 63, as said below
Outputs:
- preconditioned: bfloat16 [64, 16, 512, 512], P('dp', 'mp')
The draws below stay inside these ranges and needn't reach their ends.
Inputs may be any that keep to these rules, and one draw needn't show every extreme that they name: For each index of mp exactly 2 of its 4 statistics are refreshed (owner >= 0). The owners of the refreshed statistics, taken in order of block and side over the whole table, are consecutive numbers modulo 64, so no two are equal.
All inputs are finite; a program needn't handle non-finite values.
Results may differ from the reference program's by a relative error of at most 0.001.
The reference program's roundings to bfloat16 on the way count: a program that leaves them out, or rounds other values in their place, can miss the bound.
Values may be sent and summed in bfloat16 or wider, within the bound.
No kernel may reach another device: no remote copies, remote signals or barrier semaphores. Data moves between devices by JAX's collectives and lax.ppermute only.
A program may use at most 64 MiB of HBM per device.

```python
import math
import jax
import jax.numpy as jnp
from jax import lax

B = 512
NB = 2
ITERS = 3
LAYERS = 4
SHARDS = 64
BLOCKS = 16


def draw_grads(key, part):
    key = jax.random.fold_in(key, 11)
    subkeys = jax.random.split(key, 4)
    whole_shape = (SHARDS, BLOCKS, B, B)
    common = jnp.clip(jax.random.normal(subkeys[0], (1, BLOCKS, B, B), jnp.float32), -6.0, 6.0)
    private = jnp.clip(jax.random.normal(subkeys[1], whole_shape, jnp.float32), -6.0, 6.0)
    row_scale = jnp.exp(jax.random.uniform(subkeys[2], (1, BLOCKS, B, 1), jnp.float32) * (0.5 * math.log(10.0)))
    col_scale = jnp.exp(jax.random.uniform(subkeys[3], (1, BLOCKS, 1, B), jnp.float32) * (0.5 * math.log(10.0)))
    shard_pos = jnp.arange(SHARDS, dtype=jnp.float32) / max(SHARDS - 1, 1)
    block_pos = jnp.arange(BLOCKS, dtype=jnp.float32) / max(BLOCKS - 1, 1)
    shard_scale = jnp.exp(shard_pos * (0.5 * math.log(3.0))).reshape(SHARDS, 1, 1, 1)
    block_scale = jnp.exp(block_pos * (0.5 * math.log(3.0))).reshape(1, BLOCKS, 1, 1)
    values = shard_scale * block_scale * row_scale * col_scale * (common + private)
    return values.astype(jnp.bfloat16)


def draw_prev_roots(key, part):
    key = jax.random.fold_in(key, 23)
    subkeys = jax.random.split(key, 2)
    off_diagonal = jax.random.normal(subkeys[0], (BLOCKS, 2, B, B), jnp.float32)
    diagonal = jax.random.uniform(subkeys[1], (BLOCKS, 2, B), jnp.float32, 0.5, 1.5)
    symmetric = (off_diagonal + jnp.swapaxes(off_diagonal, 2, 3)) * (0.5 / math.sqrt(2.0 * B))
    identity = jnp.eye(B, dtype=jnp.float32)
    return (symmetric + diagonal[:, :, :, None] * identity).astype(jnp.bfloat16)


def draw_owners(key, part):
    key = jax.random.fold_in(key, 37)
    subkeys = jax.random.split(key, 2)
    columns = BLOCKS // NB
    stat_count = 2 * NB
    scores = jax.random.randint(subkeys[0], (columns, stat_count), 0, 1 << 20) * stat_count + jnp.arange(stat_count, dtype=jnp.int32)[None, :]
    order_rank = jnp.argsort(jnp.argsort(scores, axis=1), axis=1)
    refreshed = (order_rank < NB).reshape(-1)
    running = jnp.cumsum(refreshed.astype(jnp.int32)) - 1
    refreshed_total = columns * NB
    offset = jax.random.randint(subkeys[1], (), SHARDS - refreshed_total + 1, SHARDS)
    owner_table = jnp.where(refreshed, (offset + running) % SHARDS, -1)
    return owner_table.reshape(BLOCKS, 2).astype(jnp.int32)


def touch_ends(result, own_key, low, top_value):
    longest = result.shape.index(max(result.shape))
    spots = []
    for shift in (0, 1):
        where = [jax.random.randint(jax.random.fold_in(own_key, axis), (), 0, length) for axis, length in enumerate(result.shape)]
        where[longest] = (where[longest] + shift) % result.shape[longest]
        spots.append(tuple(where))
    return result.at[spots[0]].set(low).at[spots[1]].set(top_value)


def setup_inputs(seed: int = 0) -> dict:
    key_of = jax.random.split(jax.random.key(seed), 6)
    return {
        "grads": draw_grads(jax.random.fold_in(key_of[5], 71), 0),
        "prev_roots": draw_prev_roots(jax.random.fold_in(key_of[5], 71), 0),
        "damping": jnp.clip(jnp.exp(jax.random.uniform(key_of[2], (LAYERS,), jnp.float32, math.log(0.05), math.log(1.0))), 0.05, 1.0),
        "block_layer": touch_ends(jax.random.randint(key_of[3], (BLOCKS,), 0, LAYERS), jax.random.fold_in(key_of[3], 1), 0, LAYERS - 1).astype(jnp.int32),
        "owners": draw_owners(jax.random.fold_in(key_of[5], 71), 0),
    }


NORM_EPSILON = 1e-06
HIGHEST_PRECISION = lax.Precision.HIGHEST

def newton_root(statistic):
    identity = jnp.eye(B, dtype=jnp.float32)
    norm_scale = 5.0 / (2.0 * jnp.sqrt(jnp.sum(statistic * statistic)))
    mat_m = norm_scale * statistic
    mat_h = jnp.sqrt(jnp.sqrt(norm_scale)) * identity
    for iteration in range(ITERS):
        newton_step = 1.25 * identity - 0.25 * mat_m
        mat_h = jnp.dot(mat_h, newton_step, precision=HIGHEST_PRECISION, preferred_element_type=jnp.float32)
        square = jnp.dot(newton_step, newton_step, precision=HIGHEST_PRECISION, preferred_element_type=jnp.float32)
        fourth = jnp.dot(square, square, precision=HIGHEST_PRECISION, preferred_element_type=jnp.float32)
        mat_m = jnp.dot(fourth, mat_m, precision=HIGHEST_PRECISION, preferred_element_type=jnp.float32)
    return mat_h

def reference(grads, prev_roots, damping, block_layer, owners):
    flat_owner = owners.reshape(2 * BLOCKS)
    identity = jnp.eye(B, dtype=jnp.float32)

    def refresh(stat_id):
        block_id = stat_id // 2
        side_id = stat_id % 2

        def fresh_root(unused):
            blocks = lax.dynamic_index_in_dim(grads, block_id, 1, keepdims=False).astype(jnp.float32)
            oriented = jnp.where(side_id == 0, blocks, jnp.swapaxes(blocks, 1, 2))
            statistic = jnp.einsum('dik,djk->ij', oriented, oriented, precision=HIGHEST_PRECISION) / (SHARDS * B)
            mean_eigen = jnp.trace(statistic) / B
            damped = statistic + damping[block_layer[block_id]] * mean_eigen * identity
            return newton_root(damped).astype(jnp.bfloat16)

        def keep_root(unused):
            return prev_roots[block_id, side_id]
        return lax.cond(flat_owner[stat_id] >= 0, fresh_root, keep_root, 0)
    root_table = lax.map(refresh, jnp.arange(2 * BLOCKS, dtype=jnp.int32)).reshape(BLOCKS, 2, B, B)

    def precondition(block_id):
        blocks = lax.dynamic_index_in_dim(grads, block_id, 1, keepdims=False).astype(jnp.float32)
        root_pair = lax.dynamic_index_in_dim(root_table, block_id, 0, keepdims=False).astype(jnp.float32)
        half_product = jnp.einsum('ik,dkj->dij', root_pair[0], blocks, precision=HIGHEST_PRECISION)
        half_product = lax.optimization_barrier(half_product.astype(jnp.bfloat16)).astype(jnp.float32)
        update = jnp.einsum('dik,kj->dij', half_product, root_pair[1], precision=HIGHEST_PRECISION)
        return (update, lax.optimization_barrier(jnp.sum(blocks * blocks, axis=(1, 2))), lax.optimization_barrier(jnp.sum(update * update, axis=(1, 2))))
    updates, grad_sq, upd_sq = lax.map(precondition, jnp.arange(BLOCKS, dtype=jnp.int32))
    layer_match = block_layer[:, None] == jnp.arange(LAYERS, dtype=jnp.int32)[None, :]
    layer_grad = lax.optimization_barrier(jnp.sum(jnp.where(layer_match[:, :, None], grad_sq[:, None, :], 0.0), axis=0))
    layer_upd = lax.optimization_barrier(jnp.sum(jnp.where(layer_match[:, :, None], upd_sq[:, None, :], 0.0), axis=0))
    layer_ratio = jnp.sqrt((layer_grad + NORM_EPSILON) / (layer_upd + NORM_EPSILON))
    block_ratio = lax.optimization_barrier(jnp.sum(jnp.where(layer_match[:, :, None], layer_ratio[None, :, :], 0.0), axis=1))
    scaled = (updates * block_ratio[:, :, None, None]).astype(jnp.bfloat16)
    return jnp.swapaxes(scaled, 0, 1)
```

```python
import jax
import jax.numpy as jnp
from jax import lax
from jax.sharding import Mesh, PartitionSpec as P

B = 512
NB = 2
ITERS = 3
LAYERS = 4
SHARDS = 64
NORM_EPSILON = 1e-06
HIGHEST = lax.Precision.HIGHEST
PLANE = ("y", "x")
COLUMN = ("h", "c")


def mm(a, b):
    return jnp.dot(a, b, precision=HIGHEST, preferred_element_type=jnp.float32)


def newton_root(statistic):
    identity = jnp.eye(B, dtype=jnp.float32)
    norm_scale = 5.0 / (2.0 * jnp.sqrt(jnp.sum(statistic * statistic)))
    mat_m = norm_scale * statistic
    mat_h = None
    for iteration in range(ITERS):
        step = 1.25 * identity - 0.25 * mat_m
        mat_h = step if mat_h is None else mm(mat_h, step)
        if iteration + 1 < ITERS:
            square = mm(step, step)
            mat_m = mm(mm(square, square), mat_m)
    return (jnp.sqrt(jnp.sqrt(norm_scale)) * mat_h).astype(jnp.bfloat16)


def spread(a, axes, count):
    return lax.all_to_all(jnp.broadcast_to(a[None], (count,) + a.shape), axes, 0, 0)


def per_device(grads, prev_roots, damping, block_layer, owners):
    g = grads[0]
    fresh = owners.reshape(2 * NB) >= 0
    first = jnp.argmax(fresh)
    last = 2 * NB - 1 - jnp.argmax(fresh[::-1])
    layer_match = block_layer[:, None] == jnp.arange(LAYERS, dtype=jnp.int32)[None, :]
    block_damp = jnp.sum(jnp.where(layer_match, damping[None, :], 0.0), axis=1)

    def gram(stat):
        block = g[stat // 2]
        block = jnp.where(stat % 2 == 0, block, block.T)
        return jnp.dot(block, block.T, preferred_element_type=jnp.float32)

    row = lax.broadcasted_iota(jnp.int32, (B, B), 0)
    col = lax.broadcasted_iota(jnp.int32, (B, B), 1)
    gram_a, gram_b = gram(first), gram(last)
    diag_b = jnp.sum(jnp.where(row == col, gram_b, 0.0), axis=0).reshape(4, 128)
    packed = jnp.where(row >= col, gram_a, gram_b).reshape(16, 32 * 4, 128)
    packed = jnp.concatenate([packed, jnp.broadcast_to(jnp.pad(diag_b, ((0, 4), (0, 0)))[None], (16, 8, 128))], axis=1)
    part = jnp.sum(lax.all_to_all(packed, PLANE, 0, 0), axis=0)
    part = jnp.sum(spread(part, "z", 4), axis=0)
    diag_b = part[128:132].reshape(1, B)
    packed = spread(part[:128], PLANE, 16).reshape(B, B)
    flipped = packed.T
    identity = jnp.eye(B, dtype=jnp.float32)

    def root(statistic, stat):
        statistic = statistic / (SHARDS * B)
        damp = block_damp[stat // 2] * jnp.trace(statistic) / B
        return newton_root(statistic + damp * identity)

    root_a = root(jnp.where(row >= col, packed, flipped), first)
    root_b = root(jnp.where(row == col, diag_b, jnp.where(row < col, packed, flipped)), last)

    def table(block, side):
        stat = 2 * block + side
        old = prev_roots[block, side]
        return jnp.where(stat == first, root_a, jnp.where(stat == last, root_b, old))

    left = jnp.stack([table(b, 0) for b in range(NB)])
    right = jnp.stack([table(b, 1) for b in range(NB)])
    half = jnp.einsum("bik,bkj->bij", left, g, preferred_element_type=jnp.float32).astype(jnp.bfloat16)
    update = jnp.einsum("bik,bkj->bij", half, right, preferred_element_type=jnp.float32)
    grad_sq = jnp.sum(jnp.square(g.astype(jnp.float32)), axis=(1, 2))
    upd_sq = jnp.sum(update * update, axis=(1, 2))
    sums = jnp.stack([grad_sq, upd_sq])
    sums = jnp.sum(jnp.where(layer_match[None], sums[:, :, None], 0.0), axis=1)
    sums = jnp.sum(spread(jnp.pad(sums.reshape(1, 2 * LAYERS), ((0, 0), (0, 120))), COLUMN, 8), axis=0)
    sums = sums[0, : 2 * LAYERS].reshape(2, LAYERS)
    layer_ratio = jnp.sqrt((sums[0] + NORM_EPSILON) / (sums[1] + NORM_EPSILON))
    block_ratio = jnp.sum(jnp.where(layer_match, layer_ratio[None, :], 0.0), axis=1)
    return (update * block_ratio[:, None, None]).astype(jnp.bfloat16)[None]


def solution(mesh):
    dp, mp = ("z", "y", "x"), ("h", "c")
    fine = Mesh(mesh.devices.reshape(4, 4, 4, 4, 2), dp + mp)
    return jax.shard_map(
        per_device,
        mesh=fine,
        in_specs=(P(dp, mp, None, None), P(mp, None, None, None), P(), P(mp), P(mp, None)),
        out_specs=P(dp, mp, None, None),
        check_vma=False,
    )
```

```python
import jax
import jax.numpy as jnp
from jax import lax
from jax.experimental import pallas as pl
from jax.experimental.pallas import tpu as pltpu
from jax.sharding import Mesh, PartitionSpec as P

B = 512
NB = 2
LAYERS = 4
SHARDS = 64
NORM_EPSILON = 1e-06
PLANE = ("y", "x")
COLUMN = ("h", "c")
T = 128
NT = B // T
CHUNKS = 16
ROWS = B // CHUNKS
f32, bf16 = jnp.float32, jnp.bfloat16
VMEM = pl.BlockSpec(memory_space=pltpu.VMEM)
SMEM = pl.BlockSpec(memory_space=pltpu.SMEM)


def params(mib):
    return pltpu.CompilerParams(vmem_limit_bytes=mib << 20)


def dot(a, b):
    return jnp.dot(a, b, preferred_element_type=f32)


def refreshed(owners):
    f = [owners[0, 0] >= 0, owners[0, 1] >= 0, owners[1, 0] >= 0, owners[1, 1] >= 0]
    first = jnp.where(f[0], 0, jnp.where(f[1], 1, 2))
    last = jnp.where(f[3], 3, jnp.where(f[2], 2, 1))
    return first, last


def gram_kernel(owners, g, out, grams, flip):
    for slot, stat in enumerate(refreshed(owners)):
        block = g[stat // 2]

        @pl.when(stat % 2 == 0)
        def _():
            grams[slot] = lax.dot_general(block, block, (((1,), (1,)), ((), ())), preferred_element_type=f32)

        @pl.when(stat % 2 == 1)
        def _():
            flip[...] = block.T
            grams[slot] = dot(flip[...], block)

    row = lax.broadcasted_iota(jnp.int32, (ROWS, B), 0)
    col = lax.broadcasted_iota(jnp.int32, (ROWS, B), 1)
    diag = jnp.zeros((1, B), f32)
    for k in range(CHUNKS):
        rows = slice(k * ROWS, (k + 1) * ROWS)
        a, b = grams[0, rows, :], grams[1, rows, :]
        c = jnp.where(row + k * ROWS >= col, a, b)
        diag = diag + jnp.sum(jnp.where(row + k * ROWS == col, b, 0.0), axis=0, keepdims=True)
        for j in range(NT):
            out[k, j * ROWS : (j + 1) * ROWS, :] = c[:, j * T : (j + 1) * T]
    tail = jnp.concatenate([diag[:, j * T : (j + 1) * T] for j in range(NT)] + [jnp.zeros((4, T), f32)], axis=0)
    for k in range(CHUNKS):
        out[k, T : T + 8, :] = tail


def sum_kernel(parts, out):
    total = parts[0]
    for k in range(1, parts.shape[0]):
        total = total + parts[k]
    for k in range(out.shape[0]):
        out[k] = total


def plane_sum_kernel(parts, out, diag):
    total = parts[0]
    for k in range(1, parts.shape[0]):
        total = total + parts[k]
    diag[...] = total[T:]
    for k in range(out.shape[0]):
        out[k] = total[:T]


def eye_mask():
    return lax.broadcasted_iota(jnp.int32, (T, T), 0) == lax.broadcasted_iota(jnp.int32, (T, T), 1)


def tile(i, j):
    return slice(i * T, (i + 1) * T), slice(j * T, (j + 1) * T)


class Diag:
    def __init__(self, cols, rows):
        self.cols, self.rows = cols, rows

    def map(self, f):
        return Diag([f(c) for c in self.cols], [f(r) for r in self.rows])


def diag_of(blocks, mask):
    picked = [jnp.where(mask, b, 0.0) for b in blocks]
    return Diag(
        [jnp.sum(p, axis=1, keepdims=True) for p in picked],
        [jnp.sum(p, axis=0, keepdims=True) for p in picked],
    )


def split(x):
    hi = x.astype(bf16)
    return hi, (x - hi.astype(f32)).astype(bf16)


def store_right(cat, i, j, x):
    hi, lo = split(x)
    r, c = tile(i, j)
    cat[r, c] = hi
    cat[slice(r.start + B, r.stop + B), c] = lo
    cat[slice(r.start + 2 * B, r.stop + 2 * B), c] = hi


def store_left(cat, i, j, x):
    hi, lo = split(x)
    r, c = tile(i, j)
    cat[r, c] = hi
    cat[r, slice(c.start + B, c.stop + B)] = hi
    cat[r, slice(c.start + 2 * B, c.stop + 2 * B)] = lo


def finish(acc, off, diag_terms, keep, mask):
    blocks = []
    for i in range(NT):
        for j in range(NT):
            r, c = tile(i, j)
            base = acc[r, c]
            full = base + off(i, j)
            if i == j:
                full = jnp.where(mask, base + diag_terms(i), full)
                blocks.append(full)
                keep(i, j, full, jnp.where(mask, 0.0, full))
            else:
                keep(i, j, full, full)
    return diag_of(blocks, mask)


def main_kernel(owners, layers, damping, packed, diag_b, g, prev, update, sums, c_ref, m_ref, mcat, s_ref, shi, f_ref, fcat, h_ref, hcat, roots, accs):
    mask = eye_mask()
    ids = refreshed(owners)
    for k in range(CHUNKS):
        for j in range(NT):
            c_ref[k * ROWS : (k + 1) * ROWS, j * T : (j + 1) * T] = packed[k, j * ROWS : (j + 1) * ROWS, :]
    for n in range(4):
        @pl.when((ids[0] != n) & (ids[1] != n))
        def _():
            roots[n] = prev[n]
    lower = lax.broadcasted_iota(jnp.int32, (T, T), 0) >= lax.broadcasted_iota(jnp.int32, (T, T), 1)
    blocks = [{}, {}]
    diags, scales, shifts, zs = [], [], [], []
    for s in range(2):
        square = jnp.zeros((1, T), f32)
        on_diag = []
        for i in range(NT):
            for j in range(NT):
                r, c = tile(i, j)
                own = (i > j) if s == 0 else (i < j)
                if i == j:
                    b = c_ref[r, c]
                    if s == 0:
                        b = jnp.where(lower, b, b.T)
                    else:
                        b = jnp.where(mask, diag_b[i : i + 1, :], jnp.where(lower, b.T, b))
                    on_diag.append(b)
                elif own:
                    b = c_ref[r, c]
                else:
                    b = c_ref[c, r].T
                b = b * (1.0 / (SHARDS * B))
                m_ref[s, 0, r, c] = b
                square = square + jnp.sum(b * b, axis=0, keepdims=True)
        d = diag_of(on_diag, mask).map(lambda v: v * (1.0 / (SHARDS * B)))
        trace = jnp.sum(d.rows[0] + d.rows[1] + d.rows[2] + d.rows[3], axis=1, keepdims=True)
        layer = layers[ids[s] // 2]
        shift = damping[layer] * trace * (1.0 / B)
        norm = jnp.sum(square, axis=1, keepdims=True) + 2.0 * shift * trace + B * shift * shift
        z = 2.5 / jnp.sqrt(norm)
        d = d.map(lambda v: z * (v + shift))
        for i in range(NT):
            for j in range(NT):
                r, c = tile(i, j)
                b = z * m_ref[s, 0, r, c]
                m_ref[s, 0, r, c] = b
                store_right(mcat.at[s, 0], i, j, jnp.where(mask, 0.0, b) if i == j else b)
        diags.append(d)
        zs.append(z)

    def step(v):
        return 1.25 - 0.25 * v

    dm = list(diags)
    dx = [d.map(step) for d in dm]
    dh = [None, None]
    for it in range(2):
        ds, df = [None, None], [None, None]
        for s in range(2):
            left = mcat[s, it, :B, :]
            accs[s] = dot(left, left) * (1.0 / 16.0)
        for s in range(2):
            d = dx[s]

            def keep(i, j, full, bare, s=s):
                r, c = tile(i, j)
                s_ref[s, r, c] = full
                shi[s, r, c] = bare.astype(bf16)

            ds[s] = finish(
                accs.at[s],
                lambda i, j, s=s, d=d: (-0.25 * m_ref[s, it, tile(i, j)[0], tile(i, j)[1]]) * (d.cols[i] + d.rows[j]),
                lambda i, d=d: d.cols[i] * d.rows[i],
                keep,
                mask,
            )
        for s in range(2):
            accs[s] = dot(shi[s], shi[s])
        for s in range(2):
            d = ds[s]

            def keep(i, j, full, bare, s=s):
                r, c = tile(i, j)
                f_ref[s, r, c] = full
                store_left(fcat.at[s], i, j, bare)

            df[s] = finish(
                accs.at[s],
                lambda i, j, s=s, d=d: s_ref[s, tile(i, j)[0], tile(i, j)[1]] * (d.cols[i] + d.rows[j]),
                lambda i, d=d: d.cols[i] * d.rows[i],
                keep,
                mask,
            )
        for s in range(2):
            accs[s] = dot(fcat[s], mcat[s, it])
        for s in range(2):
            da, db = df[s], dm[s]

            def keep(i, j, full, bare, s=s):
                r, c = tile(i, j)
                m_ref[s, it + 1, r, c] = full
                store_right(mcat.at[s, it + 1], i, j, bare)

            dm[s] = finish(
                accs.at[s],
                lambda i, j, s=s, da=da, db=db: da.cols[i] * m_ref[s, it, tile(i, j)[0], tile(i, j)[1]]
                + f_ref[s, tile(i, j)[0], tile(i, j)[1]] * db.rows[j],
                lambda i, da=da, db=db: da.cols[i] * db.rows[i],
                keep,
                mask,
            )
        old = dx
        dx = [d.map(step) for d in dm]
        if it == 0:
            for s in range(2):
                accs[s] = dot(mcat[s, 0, :B, :], mcat[s, 1, :B, :]) * (1.0 / 16.0)
            for s in range(2):
                da, db = old[s], dx[s]

                def keep(i, j, full, bare, s=s):
                    r, c = tile(i, j)
                    h_ref[s, r, c] = full
                    store_left(hcat.at[s], i, j, bare)

                dh[s] = finish(
                    accs.at[s],
                    lambda i, j, s=s, da=da, db=db: -0.25
                    * (da.cols[i] * m_ref[s, 1, tile(i, j)[0], tile(i, j)[1]] + m_ref[s, 0, tile(i, j)[0], tile(i, j)[1]] * db.rows[j]),
                    lambda i, da=da, db=db: da.cols[i] * db.rows[i],
                    keep,
                    mask,
                )
    for s in range(2):
        accs[s] = dot(hcat[s], mcat[s, 2]) * -0.25
    for s in range(2):
        da, db = dh[s], dx[s]
        scale = jnp.sqrt(jnp.sqrt(zs[s]))

        def keep(i, j, full, bare, s=s, scale=scale):
            r, c = tile(i, j)
            roots[ids[s], r, c] = (scale * full).astype(bf16)

        finish(
            accs.at[s],
            lambda i, j, s=s, da=da, db=db: da.cols[i] * (-0.25 * m_ref[s, 2, tile(i, j)[0], tile(i, j)[1]])
            + h_ref[s, tile(i, j)[0], tile(i, j)[1]] * db.rows[j],
            lambda i, da=da, db=db: da.cols[i] * db.rows[i],
            keep,
            mask,
        )
    lane = lax.broadcasted_iota(jnp.int32, (8, T), 1)
    line = lax.broadcasted_iota(jnp.int32, (8, T), 0)
    tail = jnp.zeros((8, T), f32)
    for b in range(NB):
        half = dot(roots[2 * b], g[b]).astype(bf16)
        u = dot(half, roots[2 * b + 1])
        update[b] = u
        x = g[b].astype(f32)
        gs = jnp.sum(jnp.sum(x * x, axis=0, keepdims=True), axis=1, keepdims=True)
        us = jnp.sum(jnp.sum(u * u, axis=0, keepdims=True), axis=1, keepdims=True)
        hit = lane == layers[b]
        tail = tail + jnp.where(hit & (line == 0), gs, 0.0) + jnp.where(hit & (line == 1), us, 0.0)
    for k in range(sums.shape[0]):
        sums[k] = tail


def scale_kernel(layers, sums, update, out):
    total = sums[0]
    for k in range(1, sums.shape[0]):
        total = total + sums[k]
    ratio = jnp.sqrt((total[0:1] + NORM_EPSILON) / (total[1:2] + NORM_EPSILON))
    lane = lax.broadcasted_iota(jnp.int32, (1, T), 1)
    for b in range(NB):
        mine = jnp.sum(jnp.where(lane == layers[b], ratio, 0.0), axis=1, keepdims=True)
        out[0, b] = (update[b] * mine).astype(bf16)


def per_device(grads, prev_roots, damping, block_layer, owners):
    g = grads[0]
    prev = prev_roots.reshape(2 * NB, B, B)
    shape = jax.ShapeDtypeStruct
    packed = pl.pallas_call(
        gram_kernel,
        out_shape=shape((CHUNKS, T + 8, T), f32),
        in_specs=[SMEM, VMEM],
        out_specs=VMEM,
        scratch_shapes=[pltpu.VMEM((2, B, B), f32), pltpu.VMEM((B, B), bf16)],
        compiler_params=params(16),
        name="gram",
    )(owners, g)
    packed = lax.all_to_all(packed, PLANE, 0, 0)
    packed = pl.pallas_call(
        sum_kernel, out_shape=shape((4, T + 8, T), f32), in_specs=[VMEM], out_specs=VMEM, compiler_params=params(16), name="plane_sum"
    )(packed)
    packed = lax.all_to_all(packed, "z", 0, 0)
    packed, diag_b = pl.pallas_call(
        plane_sum_kernel,
        out_shape=[shape((CHUNKS, T, T), f32), shape((8, T), f32)],
        in_specs=[VMEM],
        out_specs=[VMEM, VMEM],
        compiler_params=params(16),
        name="line_sum",
    )(packed)
    packed = lax.all_to_all(packed, PLANE, 0, 0)
    update, sums = pl.pallas_call(
        main_kernel,
        out_shape=[shape((NB, B, B), f32), shape((8, 8, T), f32)],
        in_specs=[SMEM, SMEM, SMEM, VMEM, VMEM, VMEM, VMEM],
        out_specs=[VMEM, VMEM],
        scratch_shapes=[
            pltpu.VMEM((B, B), f32),
            pltpu.VMEM((2, 3, B, B), f32),
            pltpu.VMEM((2, 3, 3 * B, B), bf16),
            pltpu.VMEM((2, B, B), f32),
            pltpu.VMEM((2, B, B), bf16),
            pltpu.VMEM((2, B, B), f32),
            pltpu.VMEM((2, B, 3 * B), bf16),
            pltpu.VMEM((2, B, B), f32),
            pltpu.VMEM((2, B, 3 * B), bf16),
            pltpu.VMEM((4, B, B), bf16),
            pltpu.VMEM((2, B, B), f32),
        ],
        compiler_params=params(48),
        name="roots_and_update",
    )(owners, block_layer, damping, packed, diag_b, g, prev)
    sums = lax.all_to_all(sums, COLUMN, 0, 0)
    return pl.pallas_call(
        scale_kernel,
        out_shape=shape((1, NB, B, B), bf16),
        in_specs=[SMEM, VMEM, VMEM],
        out_specs=VMEM,
        compiler_params=params(16),
        name="graft",
    )(block_layer, sums, update)


def solution(mesh):
    dp, mp = ("z", "y", "x"), ("h", "c")
    fine = Mesh(mesh.devices.reshape(4, 4, 4, 4, 2), dp + mp)
    return jax.shard_map(
        per_device,
        mesh=fine,
        in_specs=(P(dp, mp, None, None), P(mp, None, None, None), P(), P(mp), P(mp, None)),
        out_specs=P(dp, mp, None, None),
        check_vma=False,
    )
```

```python
import jax
import jax.numpy as jnp
from jax import lax
from jax.experimental import pallas as pl
from jax.experimental.pallas import tpu as pltpu
from jax.sharding import Mesh, PartitionSpec as P

B = 512
NB = 2
LAYERS = 4
SHARDS = 64
NORM_EPSILON = 1e-06
PLANE = ("y", "x")
COLUMN = ("h", "c")
T = 128
NT = B // T
CHUNKS = 16
ROWS = B // CHUNKS
SPAN = 240.0
TINY = 1e-30
f32, bf16 = jnp.float32, jnp.bfloat16
VMEM = pl.BlockSpec(memory_space=pltpu.VMEM)
SMEM = pl.BlockSpec(memory_space=pltpu.SMEM)
ANY = pl.BlockSpec(memory_space=pl.ANY)


def params(mib):
    return pltpu.CompilerParams(vmem_limit_bytes=mib << 20)


def dot(a, b):
    return jnp.dot(a, b, preferred_element_type=f32)


def refreshed(owners):
    f = [owners[0, 0] >= 0, owners[0, 1] >= 0, owners[1, 0] >= 0, owners[1, 1] >= 0]
    first = jnp.where(f[0], 0, jnp.where(f[1], 1, 2))
    last = jnp.where(f[3], 3, jnp.where(f[2], 2, 1))
    return first, last


def top_of(x):
    top = jnp.max(jnp.max(jnp.abs(x), axis=0, keepdims=True), axis=1, keepdims=True)
    return jnp.maximum(top * 1.008, TINY).astype(bf16).astype(f32)


def encode(x, gain):
    size = jnp.exp2(jnp.minimum(jnp.abs(x) * gain, SPAN) - SPAN / 2)
    return jnp.where(x < 0, -size, size).astype(bf16)


def decode(code, top):
    code = code.astype(f32)
    size = (jnp.log2(jnp.abs(code)) + SPAN / 2) * top
    return jnp.where(code < 0, -size, size)


def parts3(x):
    hi = x.astype(bf16).astype(f32)
    mid = (x - hi).astype(bf16).astype(f32)
    return [hi, mid, x - hi - mid]


def tail_of(diag, top):
    return jnp.concatenate(parts3(diag) + [jnp.broadcast_to(top, (4, T))], axis=0).astype(bf16)


def read_tail(tail):
    tail = tail.astype(f32)
    return tail[0:4] + tail[4:8] + tail[8:12], tail[12:13] * (1.0 / SPAN)


def gram_kernel(owners, g_hbm, out, g, grams, flip, sems):
    copies = [pltpu.make_async_copy(g_hbm.at[0, b], g.at[b], sems.at[b]) for b in range(NB)]
    for c in copies:
        c.start()
    for c in copies:
        c.wait()
    for slot, stat in enumerate(refreshed(owners)):
        block = g[stat // 2]

        @pl.when(stat % 2 == 0)
        def _():
            grams[slot] = lax.dot_general(block, block, (((1,), (1,)), ((), ())), preferred_element_type=f32)

        @pl.when(stat % 2 == 1)
        def _():
            flip[...] = block.T
            grams[slot] = dot(flip[...], block)

    row = lax.broadcasted_iota(jnp.int32, (ROWS, B), 0)
    col = lax.broadcasted_iota(jnp.int32, (ROWS, B), 1)
    diag = [jnp.zeros((1, B), f32), jnp.zeros((1, B), f32)]
    most = [jnp.zeros((ROWS, B), f32), jnp.zeros((ROWS, B), f32)]
    for k in range(CHUNKS):
        rows = slice(k * ROWS, (k + 1) * ROWS)
        a, b = grams[0, rows, :], grams[1, rows, :]
        on = row + k * ROWS == col
        lower = row + k * ROWS > col
        upper = row + k * ROWS < col
        diag[0] = diag[0] + jnp.sum(jnp.where(on, a, 0.0), axis=0, keepdims=True)
        diag[1] = diag[1] + jnp.sum(jnp.where(on, b, 0.0), axis=0, keepdims=True)
        most[0] = jnp.maximum(most[0], jnp.where(lower, jnp.abs(a), 0.0))
        most[1] = jnp.maximum(most[1], jnp.where(upper, jnp.abs(b), 0.0))
    tops = [top_of(m) for m in most]
    gains = [SPAN / t for t in tops]
    for k in range(CHUNKS):
        rows = slice(k * ROWS, (k + 1) * ROWS)
        lower = row + k * ROWS >= col
        c = jnp.where(lower, grams[0, rows, :], grams[1, rows, :])
        c = encode(c, jnp.where(lower, gains[0], gains[1]))
        for j in range(NT):
            out[k, j * ROWS : (j + 1) * ROWS, :] = c[:, j * T : (j + 1) * T]
    tails = []
    for s in range(2):
        d = jnp.concatenate([diag[s][:, j * T : (j + 1) * T] for j in range(NT)], axis=0)
        tails.append(tail_of(d, tops[s]))
    for k in range(CHUNKS):
        out[k, T : T + 16, :] = tails[0]
        out[k, T + 16 : T + 32, :] = tails[1]


def chunk_place():
    mine = lax.axis_index("y") * 4 + lax.axis_index("x")
    r = lax.broadcasted_iota(jnp.int32, (T, T), 0)
    return mine * ROWS + r % ROWS, (r // ROWS) * T + lax.broadcasted_iota(jnp.int32, (T, T), 1)


def add_parts(parts, lower):
    total = jnp.zeros((T, T), f32)
    diag = [jnp.zeros((4, T), f32), jnp.zeros((4, T), f32)]
    for p in range(parts.shape[0]):
        da, ta = read_tail(parts[p, T : T + 16, :])
        db, tb = read_tail(parts[p, T + 16 : T + 32, :])
        total = total + decode(parts[p, :T, :], jnp.where(lower, ta, tb))
        diag = [diag[0] + da, diag[1] + db]
    return total, diag


def code_total(total, row, col):
    tops = [top_of(jnp.where(row > col, total, 0.0)), top_of(jnp.where(row < col, total, 0.0))]
    return encode(total, jnp.where(row >= col, SPAN / tops[0], SPAN / tops[1])), tops


def plane_sum_kernel(parts, out):
    row, col = chunk_place()
    total, diag = add_parts(parts, row >= col)
    code, tops = code_total(total, row, col)
    tails = [tail_of(diag[s], tops[s]) for s in range(2)]
    for k in range(out.shape[0]):
        out[k, :T, :] = code
        out[k, T : T + 16, :] = tails[0]
        out[k, T + 16 : T + 32, :] = tails[1]


def line_sum_kernel(parts, out, diag_out):
    row, col = chunk_place()
    total, diag = add_parts(parts, row >= col)
    code, tops = code_total(total, row, col)
    diag_out[0] = diag[0]
    diag_out[1] = diag[1]
    line = lax.broadcasted_iota(jnp.int32, (16, T), 0)
    tail = jnp.where(line < 8, tops[0], tops[1]).astype(bf16)
    for k in range(out.shape[0]):
        out[k, :T, :] = code
        out[k, T : T + 16, :] = tail


def tile(i, j):
    return slice(i * T, (i + 1) * T), slice(j * T, (j + 1) * T)


class Diag:
    def __init__(self, cols, rows):
        self.cols, self.rows = cols, rows

    def map(self, f):
        return Diag([f(c) for c in self.cols], [f(r) for r in self.rows])


def main_kernel(owners, layers, damping, packed, diags, g, prev, update, sums, c_ref, x_ref, xo, s_ref, so, f_ref, fo, h_ref, ho, roots, accs, sem):
    fetch = pltpu.make_async_copy(prev, roots, sem)
    fetch.start()
    row = lax.broadcasted_iota(jnp.int32, (T, T), 0)
    col = lax.broadcasted_iota(jnp.int32, (T, T), 1)
    mask = row == col
    lower = row > col
    ids = refreshed(owners)
    crow = lax.broadcasted_iota(jnp.int32, (ROWS, T), 0)
    ccol = lax.broadcasted_iota(jnp.int32, (ROWS, T), 1)
    squares = [jnp.zeros((ROWS, T), f32), jnp.zeros((ROWS, T), f32)]
    for k in range(CHUNKS):
        tail = packed[k, T : T + 16, :].astype(f32) * (1.0 / (SPAN * SHARDS * B))
        ta, tb = tail[0:1], tail[8:9]
        for j in range(NT):
            code = packed[k, j * ROWS : (j + 1) * ROWS, :]
            low, high = k * ROWS - j * T - (T - 1), k * ROWS + ROWS - 1 - j * T
            if low > 0:
                x = decode(code, ta)
                squares[0] = squares[0] + x * x
            elif high < 0:
                x = decode(code, tb)
                squares[1] = squares[1] + x * x
            else:
                r, c = crow + k * ROWS, ccol + j * T
                x = decode(code, jnp.where(r > c, ta, tb))
                x = jnp.where(r == c, 0.0, x)
                q = x * x
                squares[0] = squares[0] + jnp.where(r > c, q, 0.0)
                squares[1] = squares[1] + jnp.where(r > c, 0.0, q)
            c_ref[k * ROWS : (k + 1) * ROWS, j * T : (j + 1) * T] = x

    def total(v):
        return jnp.sum(jnp.sum(v, axis=0, keepdims=True), axis=1, keepdims=True)

    def column(r):
        return jnp.sum(jnp.where(mask, r, 0.0), axis=1, keepdims=True)

    dx, scales = [None, None], [None, None]
    for s in range(2):
        d = diags[s] * (1.0 / (SHARDS * B))
        trace = total(d)
        shift = damping[layers[ids[s] // 2]] * trace * (1.0 / B)
        d = d + shift
        z = 2.5 / jnp.sqrt(2.0 * total(squares[s]) + total(d * d))
        scales[s] = jnp.sqrt(jnp.sqrt(z))
        rows = [1.25 - 0.25 * (z * d[i : i + 1, :]) for i in range(NT)]
        dx[s] = Diag([column(r) for r in rows], rows)
        w = -0.25 * z
        for i in range(NT):
            for j in range(i + 1):
                r, c = tile(i, j)
                if i == j:
                    x = c_ref[r, c]
                    x = jnp.where(lower if s == 0 else row < col, x, x.T) * w
                    x_ref[s, 0, r, c] = x
                    xo[s, 0, r, c] = x.astype(bf16)
                else:
                    x = (c_ref[r, c] if s == 0 else c_ref[c, r]) * w
                    a, b = ((r, c), (c, r)) if s == 0 else ((c, r), (r, c))
                    x_ref[s, 0, a[0], a[1]] = x
                    xo[s, 0, a[0], a[1]] = x.astype(bf16)
                    x = x.T
                    x_ref[s, 0, b[0], b[1]] = x
                    xo[s, 0, b[0], b[1]] = x.astype(bf16)

    def finish(acc, off, da, db, keep):
        diag = Diag([], [])
        for i in range(NT):
            for j in range(NT):
                r, c = tile(i, j)
                base = acc[r, c]
                if i == j:
                    on = jnp.where(mask, base, 0.0)
                    diag.cols.append(jnp.sum(on, axis=1, keepdims=True) + da.cols[i] * db.cols[i])
                    diag.rows.append(jnp.sum(on, axis=0, keepdims=True) + da.rows[i] * db.rows[i])
                    keep(r, c, jnp.where(mask, 0.0, base + off(i, j, r, c)), diag.rows[i])
                else:
                    keep(r, c, base + off(i, j, r, c), None)
        return diag

    def square_off(d, ref):
        return lambda i, j, r, c: ref[r, c] * (d.cols[i] + d.rows[j])

    def cross_off(da, aref, db, bref):
        return lambda i, j, r, c: da.cols[i] * bref[r, c] + aref[r, c] * db.rows[j]

    def keep_in(full, off):
        def keep(r, c, x, on):
            full[r, c] = x
            off[r, c] = x.astype(bf16)

        return keep

    first = dx
    for it in range(2):
        ds, df = [None, None], [None, None]
        for s in range(2):
            accs[s] = dot(xo[s, it], xo[s, it])
            ds[s] = finish(accs.at[s], square_off(dx[s], x_ref.at[s, it]), dx[s], dx[s], keep_in(s_ref.at[s], so.at[s]))
        for s in range(2):
            accs[s] = dot(so[s], so[s])
            df[s] = finish(accs.at[s], square_off(ds[s], s_ref.at[s]), ds[s], ds[s], keep_in(f_ref.at[s], fo.at[s]))
        new = [None, None]
        for s in range(2):
            accs[s] = dot(fo[s], xo[s, it])
            dy = dx[s].map(lambda v: v - 1.25)
            new[s] = finish(
                accs.at[s], cross_off(df[s], f_ref.at[s], dy, x_ref.at[s, it]), df[s], dy, keep_in(x_ref.at[s, it + 1], xo.at[s, it + 1])
            ).map(lambda v: v + 1.25)
        dx = new
        if it == 0:
            dh = [None, None]
            for s in range(2):
                accs[s] = dot(xo[s, 0], xo[s, 1])
                dh[s] = finish(
                    accs.at[s], cross_off(first[s], x_ref.at[s, 0], dx[s], x_ref.at[s, 1]), first[s], dx[s], keep_in(h_ref.at[s], ho.at[s])
                )
    fetch.wait()
    for s in range(2):
        accs[s] = dot(ho[s], xo[s, 2])

        def keep(r, c, x, on, s=s):
            if on is not None:
                x = jnp.where(mask, on, x)
            roots[ids[s], r, c] = (x * scales[s]).astype(bf16)

        finish(accs.at[s], cross_off(dh[s], h_ref.at[s], dx[s], x_ref.at[s, 2]), dh[s], dx[s], keep)
    lane = lax.broadcasted_iota(jnp.int32, (8, T), 1)
    line = lax.broadcasted_iota(jnp.int32, (8, T), 0)
    tail = jnp.zeros((8, T), f32)
    for b in range(NB):
        half = dot(roots[2 * b], g[b]).astype(bf16)
        u = dot(half, roots[2 * b + 1])
        update[b] = u
        x = g[b].astype(f32)
        hit = lane == layers[b]
        tail = tail + jnp.where(hit & (line == 0), total(x * x), 0.0) + jnp.where(hit & (line == 1), total(u * u), 0.0)
    for k in range(sums.shape[0]):
        sums[k] = tail


def scale_kernel(layers, sums, update, out, scaled, sems):
    total = sums[0]
    for k in range(1, sums.shape[0]):
        total = total + sums[k]
    ratio = jnp.sqrt((total[0:1] + NORM_EPSILON) / (total[1:2] + NORM_EPSILON))
    lane = lax.broadcasted_iota(jnp.int32, (1, T), 1)
    copies = []
    for b in range(NB):
        mine = jnp.sum(jnp.where(lane == layers[b], ratio, 0.0), axis=1, keepdims=True)
        for h in range(2):
            rows = pl.ds(h * (B // 2), B // 2)
            scaled[b, rows, :] = (update[b, rows, :] * mine).astype(bf16)
            copies.append(pltpu.make_async_copy(scaled.at[b, rows], out.at[0, b, rows], sems.at[2 * b + h]))
            copies[-1].start()
    for c in copies:
        c.wait()


def per_device(grads, prev_roots, damping, block_layer, owners):
    prev = prev_roots.reshape(2 * NB, B, B)
    shape = jax.ShapeDtypeStruct
    packed = pl.pallas_call(
        gram_kernel,
        out_shape=shape((CHUNKS, T + 32, T), bf16),
        in_specs=[SMEM, ANY],
        out_specs=VMEM,
        scratch_shapes=[pltpu.VMEM((NB, B, B), bf16), pltpu.VMEM((2, B, B), f32), pltpu.VMEM((B, B), bf16), pltpu.SemaphoreType.DMA((NB,))],
        compiler_params=params(16),
        name="gram",
    )(owners, grads)
    packed = lax.all_to_all(packed, PLANE, 0, 0)
    packed = pl.pallas_call(
        plane_sum_kernel, out_shape=shape((4, T + 32, T), bf16), in_specs=[VMEM], out_specs=VMEM, compiler_params=params(16), name="plane_sum"
    )(packed)
    packed = lax.all_to_all(packed, "z", 0, 0)
    packed, diags = pl.pallas_call(
        line_sum_kernel,
        out_shape=[shape((CHUNKS, T + 16, T), bf16), shape((2, 4, T), f32)],
        in_specs=[VMEM],
        out_specs=[VMEM, VMEM],
        compiler_params=params(16),
        name="line_sum",
    )(packed)
    packed = lax.all_to_all(packed, PLANE, 0, 0)
    update, sums = pl.pallas_call(
        main_kernel,
        out_shape=[shape((NB, B, B), f32), shape((8, 8, T), f32)],
        in_specs=[SMEM, SMEM, SMEM, VMEM, VMEM, VMEM, ANY],
        out_specs=[VMEM, VMEM],
        scratch_shapes=[
            pltpu.VMEM((B, B), f32),
            pltpu.VMEM((2, 3, B, B), f32),
            pltpu.VMEM((2, 3, B, B), bf16),
            pltpu.VMEM((2, B, B), f32),
            pltpu.VMEM((2, B, B), bf16),
            pltpu.VMEM((2, B, B), f32),
            pltpu.VMEM((2, B, B), bf16),
            pltpu.VMEM((2, B, B), f32),
            pltpu.VMEM((2, B, B), bf16),
            pltpu.VMEM((4, B, B), bf16),
            pltpu.VMEM((2, B, B), f32),
            pltpu.SemaphoreType.DMA,
        ],
        compiler_params=params(40),
        name="roots_and_update",
    )(owners, block_layer, damping, packed, diags, grads[0], prev)
    sums = lax.all_to_all(sums, COLUMN, 0, 0)
    return pl.pallas_call(
        scale_kernel,
        out_shape=shape((1, NB, B, B), bf16),
        in_specs=[SMEM, VMEM, VMEM],
        out_specs=ANY,
        scratch_shapes=[pltpu.VMEM((NB, B, B), bf16), pltpu.SemaphoreType.DMA((2 * NB,))],
        compiler_params=params(16),
        name="graft",
    )(block_layer, sums, update)


def solution(mesh):
    dp, mp = ("z", "y", "x"), ("h", "c")
    fine = Mesh(mesh.devices.reshape(4, 4, 4, 4, 2), dp + mp)
    return jax.shard_map(
        per_device,
        mesh=fine,
        in_specs=(P(dp, mp, None, None), P(mp, None, None, None), P(), P(mp), P(mp, None)),
        out_specs=P(dp, mp, None, None),
        check_vma=False,
    )
```

```python
import jax
import jax.numpy as jnp
from jax import lax
from jax.experimental import pallas as pl
from jax.experimental.pallas import tpu as pltpu
from jax.sharding import Mesh, PartitionSpec as P

B = 512
NB = 2
LAYERS = 4
SHARDS = 64
NORM_EPSILON = 1e-06
PLANE = ("y", "x")
COLUMN = ("h", "c")
T = 128
NT = B // T
CHUNKS = 16
ROWS = B // CHUNKS
SPAN = 240.0
PIECES = 2
TINY = 1e-30
f32, bf16 = jnp.float32, jnp.bfloat16
VMEM = pl.BlockSpec(memory_space=pltpu.VMEM)
SMEM = pl.BlockSpec(memory_space=pltpu.SMEM)
ANY = pl.BlockSpec(memory_space=pltpu.HBM)


def params(mib):
    return pltpu.CompilerParams(vmem_limit_bytes=mib << 20)


def dot(a, b):
    return jnp.dot(a, b, preferred_element_type=f32)


def refreshed(owners):
    f = [owners[0, 0] >= 0, owners[0, 1] >= 0, owners[1, 0] >= 0, owners[1, 1] >= 0]
    first = jnp.where(f[0], 0, jnp.where(f[1], 1, 2))
    last = jnp.where(f[3], 3, jnp.where(f[2], 2, 1))
    return first, last


def top_of(x):
    top = jnp.max(jnp.max(jnp.abs(x), axis=0, keepdims=True), axis=1, keepdims=True)
    return jnp.maximum(top * 1.008, TINY).astype(bf16).astype(f32)


def encode(x, gain):
    size = jnp.exp2(jnp.minimum(jnp.abs(x) * gain, SPAN) - SPAN / 2)
    return jnp.where(x < 0, -size, size).astype(bf16)


def decode(code, top):
    code = code.astype(f32)
    size = (jnp.log2(jnp.abs(code)) + SPAN / 2) * top
    return jnp.where(code < 0, -size, size)


def parts3(x):
    hi = x.astype(bf16).astype(f32)
    mid = (x - hi).astype(bf16).astype(f32)
    return [hi, mid, x - hi - mid]


def tail_of(diag, top):
    return jnp.concatenate(parts3(diag) + [jnp.broadcast_to(top, (4, T))], axis=0).astype(bf16)


def read_tail(tail):
    tail = tail.astype(f32)
    return tail[0:4] + tail[4:8] + tail[8:12], tail[12:13] * (1.0 / SPAN)


def kind(k, j):
    if k * ROWS > j * T + T - 1:
        return 1
    return -1 if k * ROWS + ROWS - 1 < j * T else 0


def gram_kernel(owners_hbm, g_hbm, out, owners, g, grams, flip, sems):
    copies = [pltpu.make_async_copy(owners_hbm, owners, sems.at[NB])]
    copies += [pltpu.make_async_copy(g_hbm.at[0, b], g.at[b], sems.at[b]) for b in range(NB)]
    for c in copies:
        c.start()
    for c in copies:
        c.wait()
    for slot, stat in enumerate(refreshed(owners)):
        block = g[stat // 2]

        @pl.when(stat % 2 == 0)
        def _():
            grams[slot] = lax.dot_general(block, block, (((1,), (1,)), ((), ())), preferred_element_type=f32)

        @pl.when(stat % 2 == 1)
        def _():
            flip[...] = block.T
            grams[slot] = dot(flip[...], block)

    row = lax.broadcasted_iota(jnp.int32, (ROWS, T), 0)
    col = lax.broadcasted_iota(jnp.int32, (ROWS, T), 1)
    most = [jnp.zeros((ROWS, T), f32), jnp.zeros((ROWS, T), f32)]
    diag = [[jnp.zeros((1, T), f32) for _ in range(NT)] for _ in range(2)]
    for k in range(CHUNKS):
        rows = slice(k * ROWS, (k + 1) * ROWS)
        for j in range(NT):
            cols = slice(j * T, (j + 1) * T)
            where = kind(k, j)
            if where:
                s = (1 - where) // 2
                most[s] = jnp.maximum(most[s], jnp.abs(grams[s, rows, cols]))
            else:
                gap = row - col + (k * ROWS - j * T)
                for s in range(2):
                    x = grams[s, rows, cols]
                    diag[s][j] = diag[s][j] + jnp.sum(jnp.where(gap == 0, x, 0.0), axis=0, keepdims=True)
                    most[s] = jnp.maximum(most[s], jnp.where(gap > 0 if s == 0 else gap < 0, jnp.abs(x), 0.0))
    tops = [top_of(m) for m in most]
    gains = [SPAN / t for t in tops]
    tails = [tail_of(jnp.concatenate(diag[s], axis=0), tops[s]) for s in range(2)]
    for k in range(CHUNKS):
        rows = slice(k * ROWS, (k + 1) * ROWS)
        for j in range(NT):
            cols = slice(j * T, (j + 1) * T)
            where = kind(k, j)
            if where:
                s = (1 - where) // 2
                code = encode(grams[s, rows, cols], gains[s])
            else:
                lower = row + k * ROWS >= col + j * T
                code = encode(jnp.where(lower, grams[0, rows, cols], grams[1, rows, cols]), jnp.where(lower, gains[0], gains[1]))
            out[k, j * ROWS : (j + 1) * ROWS, :] = code
        out[k, T : T + 16, :] = tails[0]
        out[k, T + 16 : T + 32, :] = tails[1]


def chunk_place():
    mine = lax.axis_index("y") * 4 + lax.axis_index("x")
    r = lax.broadcasted_iota(jnp.int32, (T, T), 0)
    return mine * ROWS + r % ROWS, (r // ROWS) * T + lax.broadcasted_iota(jnp.int32, (T, T), 1)


def add_parts(parts, lower):
    total = jnp.zeros((T, T), f32)
    diag = [jnp.zeros((4, T), f32), jnp.zeros((4, T), f32)]
    for p in range(parts.shape[0]):
        da, ta = read_tail(parts[p, T : T + 16, :])
        db, tb = read_tail(parts[p, T + 16 : T + 32, :])
        total = total + decode(parts[p, :T, :], jnp.where(lower, ta, tb))
        diag = [diag[0] + da, diag[1] + db]
    return total, diag


def code_total(total, row, col):
    tops = [top_of(jnp.where(row > col, total, 0.0)), top_of(jnp.where(row < col, total, 0.0))]
    return encode(total, jnp.where(row >= col, SPAN / tops[0], SPAN / tops[1])), tops


def plane_sum_kernel(parts, out):
    row, col = chunk_place()
    total, diag = add_parts(parts, row >= col)
    code, tops = code_total(total, row, col)
    tails = [tail_of(diag[s], tops[s]) for s in range(2)]
    for k in range(out.shape[0]):
        out[k, :T, :] = code
        out[k, T : T + 16, :] = tails[0]
        out[k, T + 16 : T + 32, :] = tails[1]


def line_sum_kernel(parts, out, diag_out):
    row, col = chunk_place()
    total, diag = add_parts(parts, row >= col)
    code, tops = code_total(total, row, col)
    diag_out[0] = diag[0]
    diag_out[1] = diag[1]
    line = lax.broadcasted_iota(jnp.int32, (16, T), 0)
    tail = jnp.where(line < 8, tops[0], tops[1]).astype(bf16)
    for k in range(out.shape[0]):
        out[k, :T, :] = code
        out[k, T : T + 16, :] = tail


def tile(i, j):
    return slice(i * T, (i + 1) * T), slice(j * T, (j + 1) * T)


class Diag:
    def __init__(self, cols, rows):
        self.cols, self.rows = cols, rows

    def map(self, f):
        return Diag([f(c) for c in self.cols], [f(r) for r in self.rows])


def main_kernel(owners_hbm, layers_hbm, damping_hbm, packed, diags, g, prev, update, sums, hot, owners, layers, damping, sems, c_ref, x_ref, xo, s_ref, so, f_ref, fo, h_ref, ho, roots, accs):
    copies = [
        pltpu.make_async_copy(owners_hbm, owners, sems.at[0]),
        pltpu.make_async_copy(layers_hbm, layers, sems.at[1]),
        pltpu.make_async_copy(damping_hbm, damping, sems.at[2]),
    ]
    for c in copies:
        c.start()
    row = lax.broadcasted_iota(jnp.int32, (T, T), 0)
    col = lax.broadcasted_iota(jnp.int32, (T, T), 1)
    mask = row == col
    lower = row > col
    crow = lax.broadcasted_iota(jnp.int32, (ROWS, T), 0)
    ccol = lax.broadcasted_iota(jnp.int32, (ROWS, T), 1)
    squares = [jnp.zeros((ROWS, T), f32), jnp.zeros((ROWS, T), f32)]
    for k in range(CHUNKS):
        tail = packed[k, T : T + 16, :].astype(f32) * (1.0 / (SPAN * SHARDS * B))
        ta, tb = tail[0:1], tail[8:9]
        for j in range(NT):
            code = packed[k, j * ROWS : (j + 1) * ROWS, :]
            low, high = k * ROWS - j * T - (T - 1), k * ROWS + ROWS - 1 - j * T
            if low > 0:
                x = decode(code, ta)
                squares[0] = squares[0] + x * x
            elif high < 0:
                x = decode(code, tb)
                squares[1] = squares[1] + x * x
            else:
                r, c = crow + k * ROWS, ccol + j * T
                x = decode(code, jnp.where(r > c, ta, tb))
                x = jnp.where(r == c, 0.0, x)
                q = x * x
                squares[0] = squares[0] + jnp.where(r > c, q, 0.0)
                squares[1] = squares[1] + jnp.where(r > c, 0.0, q)
            c_ref[k * ROWS : (k + 1) * ROWS, j * T : (j + 1) * T] = x

    for c in copies:
        c.wait()
    ids = refreshed(owners)
    for n in range(2 * NB):

        @pl.when((ids[0] != n) & (ids[1] != n))
        def _():
            roots[n] = prev[n]

    def total(v):
        return jnp.sum(jnp.sum(v, axis=0, keepdims=True), axis=1, keepdims=True)

    def column(r):
        return jnp.sum(jnp.where(mask, r, 0.0), axis=1, keepdims=True)

    dx, scales = [None, None], [None, None]
    for s in range(2):
        d = diags[s] * (1.0 / (SHARDS * B))
        trace = total(d)
        shift = damping[layers[ids[s] // 2]] * trace * (1.0 / B)
        d = d + shift
        z = 2.5 / jnp.sqrt(2.0 * total(squares[s]) + total(d * d))
        scales[s] = jnp.sqrt(jnp.sqrt(z))
        rows = [1.25 - 0.25 * (z * d[i : i + 1, :]) for i in range(NT)]
        dx[s] = Diag([column(r) for r in rows], rows)
        w = -0.25 * z
        for i in range(NT):
            for j in range(i + 1):
                r, c = tile(i, j)
                if i == j:
                    x = c_ref[r, c]
                    x = jnp.where(lower if s == 0 else row < col, x, x.T) * w
                    x_ref[s, 0, r, c] = x
                    xo[s, 0, r, c] = x.astype(bf16)
                else:
                    x = (c_ref[r, c] if s == 0 else c_ref[c, r]) * w
                    a, b = ((r, c), (c, r)) if s == 0 else ((c, r), (r, c))
                    x_ref[s, 0, a[0], a[1]] = x
                    xo[s, 0, a[0], a[1]] = x.astype(bf16)
                    x = x.T
                    x_ref[s, 0, b[0], b[1]] = x
                    xo[s, 0, b[0], b[1]] = x.astype(bf16)

    def finish(acc, off, da, db, keep, diag):
        for j in range(NT):
            for i in range(NT if j >= NT // 2 else NT // 2):
                r, c = tile(i, j)
                base = acc[r, c]
                if i == j:
                    on = jnp.where(mask, base, 0.0)
                    diag.cols.append(jnp.sum(on, axis=1, keepdims=True) + da.cols[i] * db.cols[i])
                    diag.rows.append(jnp.sum(on, axis=0, keepdims=True) + da.rows[i] * db.rows[i])
                    keep(r, c, jnp.where(mask, 0.0, base + off(i, j, r, c)), diag.rows[i])
                else:
                    x = base + off(i, j, r, c)
                    keep(r, c, x, None)
                    if j >= NT // 2 and i < NT // 2:
                        keep(c, r, x.T, None)
            if j % 2:
                yield

    def product(acc, a, b):
        left, right = slice(0, B // 2), slice(B // 2, B)
        acc[left, left] = dot(a[left, :], b[:, left])
        yield
        acc[:, right] = dot(a[...], b[:, right])
        yield

    def together(*steps):
        steps = list(steps)
        while steps:
            steps = [st for st in steps if next(st, steps) is not steps]

    def square_off(d, ref):
        return lambda i, j, r, c: ref[r, c] * (d.cols[i] + d.rows[j])

    def cross_off(da, aref, db, bref):
        return lambda i, j, r, c: da.cols[i] * bref[r, c] + aref[r, c] * db.rows[j]

    def keep_in(full, off):
        def keep(r, c, x, on):
            full[r, c] = x
            off[r, c] = x.astype(bf16)

        return keep

    def newton(s):
        x = [dx[s]]
        for it in range(2):
            d = x[it]
            ds, df, dn = Diag([], []), Diag([], []), Diag([], [])
            yield product(accs.at[s], xo.at[s, it], xo.at[s, it]), finish(accs.at[s], square_off(d, x_ref.at[s, it]), d, d, keep_in(s_ref.at[s], so.at[s]), ds)
            yield product(accs.at[s], so.at[s], so.at[s]), finish(accs.at[s], square_off(ds, s_ref.at[s]), ds, ds, keep_in(f_ref.at[s], fo.at[s]), df)
            dy = d.map(lambda v: v - 1.25)
            yield (
                product(accs.at[s], fo.at[s], xo.at[s, it]),
                finish(accs.at[s], cross_off(df, f_ref.at[s], dy, x_ref.at[s, it]), df, dy, keep_in(x_ref.at[s, it + 1], xo.at[s, it + 1]), dn),
            )
            x.append(dn.map(lambda v: v + 1.25))
            if it == 0:
                dh = Diag([], [])
                yield (
                    product(accs.at[s], xo.at[s, 0], xo.at[s, 1]),
                    finish(accs.at[s], cross_off(x[0], x_ref.at[s, 0], x[1], x_ref.at[s, 1]), x[0], x[1], keep_in(h_ref.at[s], ho.at[s]), dh),
                )

        def keep(r, c, v, on):
            if on is not None:
                v = jnp.where(mask, on, v)
            roots[ids[s], r, c] = (v * scales[s]).astype(bf16)

        yield (
            product(accs.at[s], ho.at[s], xo.at[s, 2]),
            finish(accs.at[s], cross_off(dh, h_ref.at[s], x[2], x_ref.at[s, 2]), dh, x[2], keep, Diag([], [])),
        )

    chains = [newton(0), newton(1)]
    waiting = None
    for turn in range(16):
        work, rest = next(chains[turn % 2])
        together(*([work] if waiting is None else [work, waiting]))
        waiting = rest
    together(waiting)
    lane = lax.broadcasted_iota(jnp.int32, (8, T), 1)
    line = lax.broadcasted_iota(jnp.int32, (8, T), 0)
    tail = jnp.zeros((8, T), f32)
    ones = jnp.zeros((8, T), f32)
    for b in range(NB):
        ones = jnp.where((lane == layers[b]) & (line == b), 1.0, ones)
    hot[...] = ones
    for b in range(NB):
        half = dot(roots[2 * b], g[b]).astype(bf16)
        u = dot(half, roots[2 * b + 1])
        update[b] = u
        x = g[b].astype(f32)
        hit = lane == layers[b]
        tail = tail + jnp.where(hit & (line == 0), total(x * x), 0.0) + jnp.where(hit & (line == 1), total(u * u), 0.0)
    for k in range(sums.shape[0]):
        sums[k] = tail


def scale_kernel(hot, sums, update, out, scaled, sems):
    total = sums[0]
    for k in range(1, sums.shape[0]):
        total = total + sums[k]
    ratio = jnp.sqrt((total[0:1] + NORM_EPSILON) / (total[1:2] + NORM_EPSILON))
    copies = []
    for b in range(NB):
        mine = jnp.sum(hot[b : b + 1] * ratio, axis=1, keepdims=True)
        for h in range(PIECES):
            rows = pl.ds(h * (B // PIECES), B // PIECES)
            scaled[b, rows, :] = (update[b, rows, :] * mine).astype(bf16)
            copies.append(pltpu.make_async_copy(scaled.at[b, rows], out.at[0, b, rows], sems.at[b, h]))
            copies[-1].start()
    for c in copies:
        c.wait()


shape = jax.ShapeDtypeStruct


def gram_call(owners, grads):
    return pl.pallas_call(
        gram_kernel,
        out_shape=shape((CHUNKS, T + 32, T), bf16),
        in_specs=[ANY, ANY],
        out_specs=VMEM,
        scratch_shapes=[
            pltpu.SMEM((NB, 2), jnp.int32),
            pltpu.VMEM((NB, B, B), bf16),
            pltpu.VMEM((2, B, B), f32),
            pltpu.VMEM((B, B), bf16),
            pltpu.SemaphoreType.DMA((NB + 1,)),
        ],
        compiler_params=params(53),
        name="gram",
    )(owners, grads)


def plane_call(packed):
    return pl.pallas_call(
        plane_sum_kernel, out_shape=shape((4, T + 32, T), bf16), in_specs=[VMEM], out_specs=VMEM, compiler_params=params(16), name="plane_sum"
    )(packed)


def line_call(packed):
    return pl.pallas_call(
        line_sum_kernel,
        out_shape=[shape((CHUNKS, T + 16, T), bf16), shape((2, 4, T), f32)],
        in_specs=[VMEM],
        out_specs=[VMEM, VMEM],
        compiler_params=params(16),
        name="line_sum",
    )(packed)


def roots_call(owners, block_layer, damping, packed, diags, grads, prev):
    return pl.pallas_call(
        main_kernel,
        out_shape=[shape((NB, B, B), f32), shape((8, 8, T), f32), shape((8, T), f32)],
        in_specs=[ANY, ANY, ANY, VMEM, VMEM, VMEM, VMEM],
        out_specs=[VMEM, VMEM, VMEM],
        scratch_shapes=[
            pltpu.SMEM((NB, 2), jnp.int32),
            pltpu.SMEM((NB,), jnp.int32),
            pltpu.SMEM((LAYERS,), f32),
            pltpu.SemaphoreType.DMA((3,)),
            pltpu.VMEM((B, B), f32),
            pltpu.VMEM((2, 3, B, B), f32),
            pltpu.VMEM((2, 3, B, B), bf16),
            pltpu.VMEM((2, B, B), f32),
            pltpu.VMEM((2, B, B), bf16),
            pltpu.VMEM((2, B, B), f32),
            pltpu.VMEM((2, B, B), bf16),
            pltpu.VMEM((2, B, B), f32),
            pltpu.VMEM((2, B, B), bf16),
            pltpu.VMEM((4, B, B), bf16),
            pltpu.VMEM((2, B, B), f32),
        ],
        compiler_params=params(40),
        name="roots_and_update",
    )(owners, block_layer, damping, packed, diags, grads[0], prev)


def graft_call(hot, sums, update):
    return pl.pallas_call(
        scale_kernel,
        out_shape=shape((1, NB, B, B), bf16),
        in_specs=[VMEM, VMEM, VMEM],
        out_specs=ANY,
        scratch_shapes=[pltpu.VMEM((NB, B, B), bf16), pltpu.SemaphoreType.DMA((NB, PIECES))],
        compiler_params=params(16),
        name="graft",
    )(hot, sums, update)


def per_device(grads, prev_roots, damping, block_layer, owners):
    packed = lax.all_to_all(gram_call(owners, grads), PLANE, 0, 0)
    packed = lax.all_to_all(plane_call(packed), "z", 0, 0)
    packed, diags = line_call(packed)
    packed = lax.all_to_all(packed, PLANE, 0, 0)
    update, sums, hot = roots_call(owners, block_layer, damping, packed, diags, grads, prev_roots.reshape(2 * NB, B, B))
    return graft_call(hot, lax.all_to_all(sums, COLUMN, 0, 0), update)


def solution(mesh):
    dp, mp = ("z", "y", "x"), ("h", "c")
    fine = Mesh(mesh.devices.reshape(4, 4, 4, 4, 2), dp + mp)
    return jax.shard_map(
        per_device,
        mesh=fine,
        in_specs=(P(dp, mp, None, None), P(mp, None, None, None), P(), P(mp), P(mp, None)),
        out_specs=P(dp, mp, None, None),
        check_vma=False,
    )
```

```python
import math

import jax
import jax.numpy as jnp
from jax import lax
from jax.experimental import pallas as pl
from jax.experimental.pallas import tpu as pltpu
from jax.sharding import Mesh, PartitionSpec as P

B = 512
NB = 2
LAYERS = 4
SHARDS = 64
NORM_EPSILON = 1e-06
PLANE = ("y", "x")
COLUMN = ("h", "c")
T = 128
NT = B // T
CHUNKS = 16
ROWS = B // CHUNKS
SPAN = 240.0
HALF = SPAN / 2 * math.log(2.0)
UNIT = 1.0 / (SPAN * math.log(2.0))
PIECES = 2
TAIL = 16
TINY = 1e-30
f32, bf16 = jnp.float32, jnp.bfloat16
VMEM = pl.BlockSpec(memory_space=pltpu.VMEM)
SMEM = pl.BlockSpec(memory_space=pltpu.SMEM)
ANY = pl.BlockSpec(memory_space=pltpu.HBM)


def params(mib):
    return pltpu.CompilerParams(vmem_limit_bytes=mib << 20)


def dot(a, b):
    return jnp.dot(a, b, preferred_element_type=f32)


def refreshed(owners):
    f = [owners[0, 0] >= 0, owners[0, 1] >= 0, owners[1, 0] >= 0, owners[1, 1] >= 0]
    first = jnp.where(f[0], 0, jnp.where(f[1], 1, 2))
    last = jnp.where(f[3], 3, jnp.where(f[2], 2, 1))
    return first, last


def top_of(x):
    top = jnp.max(jnp.max(jnp.abs(x), axis=0, keepdims=True), axis=1, keepdims=True)
    return jnp.maximum(top * 1.008, TINY).astype(bf16).astype(f32)


def encode(x, gain):
    size = jnp.exp2(jnp.minimum(jnp.abs(x) * gain, SPAN) - SPAN / 2)
    return jnp.where(x < 0, -size, size).astype(bf16)


def decode(code, top):
    code = code.astype(f32)
    size = (jnp.log(jnp.abs(code)) + HALF) * top
    return jnp.where(code < 0, -size, size)


def parts3(x):
    hi = x.astype(bf16).astype(f32)
    mid = (x - hi).astype(bf16).astype(f32)
    return [hi, mid, x - hi - mid]


def tail_of(diags, tops):
    rows = parts3(diags[0]) + parts3(diags[1]) + [jnp.broadcast_to(t, (1, T)) for t in tops]
    return jnp.concatenate(rows + [jnp.zeros((8, T), f32)], axis=0).astype(bf16)


def read_tail(tail):
    t = tail.astype(f32)
    return [t[0:1] + t[1:2] + t[2:3], t[3:4] + t[4:5] + t[5:6]], [t[6:7] * UNIT, t[7:8] * UNIT]


def kind(k, j):
    if k * ROWS > j * T + T - 1:
        return 1
    return -1 if k * ROWS + ROWS - 1 < j * T else 0


def gram_kernel(owners_hbm, g_hbm, out, owners, g, grams, flip, sems):
    copies = [pltpu.make_async_copy(owners_hbm, owners, sems.at[NB])]
    copies += [pltpu.make_async_copy(g_hbm.at[0, b], g.at[b], sems.at[b]) for b in range(NB)]
    for c in copies:
        c.start()
    for c in copies:
        c.wait()
    for slot, stat in enumerate(refreshed(owners)):
        block = g[stat // 2]

        @pl.when(stat % 2 == 0)
        def _():
            grams[slot] = lax.dot_general(block, block, (((1,), (1,)), ((), ())), preferred_element_type=f32)

        @pl.when(stat % 2 == 1)
        def _():
            flip[...] = block.T
            grams[slot] = dot(flip[...], block)

    row = lax.broadcasted_iota(jnp.int32, (ROWS, T), 0)
    col = lax.broadcasted_iota(jnp.int32, (ROWS, T), 1)
    most = [jnp.zeros((ROWS, T), f32), jnp.zeros((ROWS, T), f32)]
    diag = [[jnp.zeros((1, T), f32) for _ in range(NT)] for _ in range(2)]
    for k in range(CHUNKS):
        rows = slice(k * ROWS, (k + 1) * ROWS)
        for j in range(NT):
            cols = slice(j * T, (j + 1) * T)
            where = kind(k, j)
            if where:
                s = (1 - where) // 2
                most[s] = jnp.maximum(most[s], jnp.abs(grams[s, rows, cols]))
            else:
                gap = row - col + (k * ROWS - j * T)
                for s in range(2):
                    x = grams[s, rows, cols]
                    diag[s][j] = diag[s][j] + jnp.sum(jnp.where(gap == 0, x, 0.0), axis=0, keepdims=True)
                    most[s] = jnp.maximum(most[s], jnp.where(gap > 0 if s == 0 else gap < 0, jnp.abs(x), 0.0))
    tops = [top_of(m) for m in most]
    gains = [SPAN / t for t in tops]
    tails = [tail_of([diag[0][j], diag[1][j]], tops) for j in range(NT)]
    for k in range(CHUNKS):
        rows = slice(k * ROWS, (k + 1) * ROWS)
        for j in range(NT):
            cols = slice(j * T, (j + 1) * T)
            where = kind(k, j)
            if where:
                s = (1 - where) // 2
                code = encode(grams[s, rows, cols], gains[s])
            else:
                lower = row + k * ROWS >= col + j * T
                code = encode(jnp.where(lower, grams[0, rows, cols], grams[1, rows, cols]), jnp.where(lower, gains[0], gains[1]))
            out[k, j * ROWS : (j + 1) * ROWS, :] = code
        out[k, T : T + TAIL, :] = tails[k * ROWS // T]


def chunk_place():
    mine = lax.axis_index("y") * 4 + lax.axis_index("x")
    r = lax.broadcasted_iota(jnp.int32, (T, T), 0)
    return mine * ROWS + r % ROWS, (r // ROWS) * T + lax.broadcasted_iota(jnp.int32, (T, T), 1)


def add_parts(parts, lower):
    total = jnp.zeros((T, T), f32)
    diag = [jnp.zeros((1, T), f32), jnp.zeros((1, T), f32)]
    for p in range(parts.shape[0]):
        d, tops = read_tail(parts[p, T : T + TAIL, :])
        total = total + decode(parts[p, :T, :], jnp.where(lower, tops[0], tops[1]))
        diag = [diag[0] + d[0], diag[1] + d[1]]
    return total, diag


def code_total(total, row, col):
    tops = [top_of(jnp.where(row > col, total, 0.0)), top_of(jnp.where(row < col, total, 0.0))]
    return encode(total, jnp.where(row >= col, SPAN / tops[0], SPAN / tops[1])), tops


def sum_kernel(parts, out):
    row, col = chunk_place()
    total, diag = add_parts(parts, row >= col)
    code, tops = code_total(total, row, col)
    tail = tail_of(diag, tops)
    for k in range(out.shape[0]):
        out[k, :T, :] = code
        out[k, T : T + TAIL, :] = tail


def tile(i, j):
    return slice(i * T, (i + 1) * T), slice(j * T, (j + 1) * T)


class Diag:
    def __init__(self, cols, rows):
        self.cols, self.rows = cols, rows

    def map(self, f):
        return Diag([f(c) for c in self.cols], [f(r) for r in self.rows])


def main_kernel(owners_hbm, layers_hbm, damping_hbm, packed, g, prev, update, sums, hot, owners, layers, damping, sems, c_ref, x_ref, xo, s_ref, so, f_ref, fo, h_ref, ho, roots, accs):
    copies = [
        pltpu.make_async_copy(owners_hbm, owners, sems.at[0]),
        pltpu.make_async_copy(layers_hbm, layers, sems.at[1]),
        pltpu.make_async_copy(damping_hbm, damping, sems.at[2]),
    ]
    for c in copies:
        c.start()
    row = lax.broadcasted_iota(jnp.int32, (T, T), 0)
    col = lax.broadcasted_iota(jnp.int32, (T, T), 1)
    mask = row == col
    lower = row > col
    crow = lax.broadcasted_iota(jnp.int32, (ROWS, T), 0)
    ccol = lax.broadcasted_iota(jnp.int32, (ROWS, T), 1)
    squares = [jnp.zeros((ROWS, T), f32), jnp.zeros((ROWS, T), f32)]
    diags = [[], []]
    for k in range(CHUNKS):
        pieces, tops = read_tail(packed[k, T : T + TAIL, :])
        ta, tb = [t * (1.0 / (SHARDS * B)) for t in tops]
        if k * ROWS % T == 0:
            for s in range(2):
                diags[s].append(pieces[s] * (1.0 / (SHARDS * B)))
        for j in range(NT):
            code = packed[k, j * ROWS : (j + 1) * ROWS, :]
            low, high = k * ROWS - j * T - (T - 1), k * ROWS + ROWS - 1 - j * T
            if low > 0:
                x = decode(code, ta)
                squares[0] = squares[0] + x * x
            elif high < 0:
                x = decode(code, tb)
                squares[1] = squares[1] + x * x
            else:
                r, c = crow + k * ROWS, ccol + j * T
                x = decode(code, jnp.where(r > c, ta, tb))
                x = jnp.where(r == c, 0.0, x)
                q = x * x
                squares[0] = squares[0] + jnp.where(r > c, q, 0.0)
                squares[1] = squares[1] + jnp.where(r > c, 0.0, q)
            c_ref[k * ROWS : (k + 1) * ROWS, j * T : (j + 1) * T] = x

    for c in copies:
        c.wait()
    ids = refreshed(owners)
    for n in range(2 * NB):

        @pl.when((ids[0] != n) & (ids[1] != n))
        def _():
            roots[n] = prev[n]

    def total(v):
        return jnp.sum(jnp.sum(v, axis=0, keepdims=True), axis=1, keepdims=True)

    def column(r):
        return jnp.sum(jnp.where(mask, r, 0.0), axis=1, keepdims=True)

    dx, scales = [None, None], [None, None]
    for s in range(2):
        d = jnp.concatenate(diags[s], axis=0)
        trace = total(d)
        shift = damping[layers[ids[s] // 2]] * trace * (1.0 / B)
        d = d + shift
        z = 2.5 / jnp.sqrt(2.0 * total(squares[s]) + total(d * d))
        scales[s] = jnp.sqrt(jnp.sqrt(z))
        rows = [1.25 - 0.25 * (z * d[i : i + 1, :]) for i in range(NT)]
        dx[s] = Diag([column(r) for r in rows], rows)
        w = -0.25 * z
        for i in range(NT):
            for j in range(i + 1):
                r, c = tile(i, j)
                if i == j:
                    x = c_ref[r, c]
                    x = jnp.where(lower if s == 0 else row < col, x, x.T) * w
                    x_ref[s, 0, r, c] = x
                    xo[s, 0, r, c] = x.astype(bf16)
                else:
                    x = (c_ref[r, c] if s == 0 else c_ref[c, r]) * w
                    a, b = ((r, c), (c, r)) if s == 0 else ((c, r), (r, c))
                    x_ref[s, 0, a[0], a[1]] = x
                    xo[s, 0, a[0], a[1]] = x.astype(bf16)
                    x = x.T
                    x_ref[s, 0, b[0], b[1]] = x
                    xo[s, 0, b[0], b[1]] = x.astype(bf16)

    def finish(acc, off, da, db, keep, diag):
        for j in range(NT):
            for i in range(NT if j >= NT // 2 else NT // 2):
                r, c = tile(i, j)
                base = acc[r, c]
                if i == j:
                    on = jnp.where(mask, base, 0.0)
                    diag.cols.append(jnp.sum(on, axis=1, keepdims=True) + da.cols[i] * db.cols[i])
                    diag.rows.append(jnp.sum(on, axis=0, keepdims=True) + da.rows[i] * db.rows[i])
                    keep(r, c, jnp.where(mask, 0.0, base + off(i, j, r, c)), diag.rows[i])
                else:
                    x = base + off(i, j, r, c)
                    keep(r, c, x, None)
                    if j >= NT // 2 and i < NT // 2:
                        keep(c, r, x.T, None)
            if j % 2:
                yield

    def product(acc, a, b):
        left, right = slice(0, B // 2), slice(B // 2, B)
        acc[left, left] = dot(a[left, :], b[:, left])
        yield
        acc[:, right] = dot(a[...], b[:, right])
        yield

    def together(*steps):
        steps = list(steps)
        while steps:
            steps = [st for st in steps if next(st, steps) is not steps]

    def square_off(d, ref):
        return lambda i, j, r, c: ref[r, c] * (d.cols[i] + d.rows[j])

    def cross_off(da, aref, db, bref):
        return lambda i, j, r, c: da.cols[i] * bref[r, c] + aref[r, c] * db.rows[j]

    def keep_in(full, off):
        def keep(r, c, x, on):
            full[r, c] = x
            off[r, c] = x.astype(bf16)

        return keep

    def newton(s):
        x = [dx[s]]
        for it in range(2):
            d = x[it]
            ds, df, dn = Diag([], []), Diag([], []), Diag([], [])
            yield product(accs.at[s], xo.at[s, it], xo.at[s, it]), finish(accs.at[s], square_off(d, x_ref.at[s, it]), d, d, keep_in(s_ref.at[s], so.at[s]), ds)
            yield product(accs.at[s], so.at[s], so.at[s]), finish(accs.at[s], square_off(ds, s_ref.at[s]), ds, ds, keep_in(f_ref.at[s], fo.at[s]), df)
            dy = d.map(lambda v: v - 1.25)
            yield (
                product(accs.at[s], fo.at[s], xo.at[s, it]),
                finish(accs.at[s], cross_off(df, f_ref.at[s], dy, x_ref.at[s, it]), df, dy, keep_in(x_ref.at[s, it + 1], xo.at[s, it + 1]), dn),
            )
            x.append(dn.map(lambda v: v + 1.25))
            if it == 0:
                dh = Diag([], [])
                yield (
                    product(accs.at[s], xo.at[s, 0], xo.at[s, 1]),
                    finish(accs.at[s], cross_off(x[0], x_ref.at[s, 0], x[1], x_ref.at[s, 1]), x[0], x[1], keep_in(h_ref.at[s], ho.at[s]), dh),
                )

        def keep(r, c, v, on):
            if on is not None:
                v = jnp.where(mask, on, v)
            roots[ids[s], r, c] = (v * scales[s]).astype(bf16)

        yield (
            product(accs.at[s], ho.at[s], xo.at[s, 2]),
            finish(accs.at[s], cross_off(dh, h_ref.at[s], x[2], x_ref.at[s, 2]), dh, x[2], keep, Diag([], [])),
        )

    chains = [newton(0), newton(1)]
    waiting = None
    for turn in range(16):
        work, rest = next(chains[turn % 2])
        together(*([work] if waiting is None else [work, waiting]))
        waiting = rest
    together(waiting)
    lane = lax.broadcasted_iota(jnp.int32, (8, T), 1)
    line = lax.broadcasted_iota(jnp.int32, (8, T), 0)
    tail = jnp.zeros((8, T), f32)
    ones = jnp.zeros((8, T), f32)
    for b in range(NB):
        ones = jnp.where((lane == layers[b]) & (line == b), 1.0, ones)
    hot[...] = ones
    for b in range(NB):
        half = dot(roots[2 * b], g[b]).astype(bf16)
        u = dot(half, roots[2 * b + 1])
        update[b] = u
        x = g[b].astype(f32)
        hit = lane == layers[b]
        tail = tail + jnp.where(hit & (line == 0), total(x * x), 0.0) + jnp.where(hit & (line == 1), total(u * u), 0.0)
    for k in range(sums.shape[0]):
        sums[k] = tail


def scale_kernel(hot, sums, update, out, scaled, sems):
    total = sums[0]
    for k in range(1, sums.shape[0]):
        total = total + sums[k]
    ratio = jnp.sqrt((total[0:1] + NORM_EPSILON) / (total[1:2] + NORM_EPSILON))
    copies = []
    for b in range(NB):
        mine = jnp.sum(hot[b : b + 1] * ratio, axis=1, keepdims=True)
        for h in range(PIECES):
            rows = pl.ds(h * (B // PIECES), B // PIECES)
            scaled[b, rows, :] = (update[b, rows, :] * mine).astype(bf16)
            copies.append(pltpu.make_async_copy(scaled.at[b, rows], out.at[0, b, rows], sems.at[b, h]))
            copies[-1].start()
    for c in copies:
        c.wait()


shape = jax.ShapeDtypeStruct


def gram_call(owners, grads):
    return pl.pallas_call(
        gram_kernel,
        out_shape=shape((CHUNKS, T + TAIL, T), bf16),
        in_specs=[ANY, ANY],
        out_specs=VMEM,
        scratch_shapes=[
            pltpu.SMEM((NB, 2), jnp.int32),
            pltpu.VMEM((NB, B, B), bf16),
            pltpu.VMEM((2, B, B), f32),
            pltpu.VMEM((B, B), bf16),
            pltpu.SemaphoreType.DMA((NB + 1,)),
        ],
        compiler_params=params(53),
        name="gram",
    )(owners, grads)


def sum_call(packed, copies, name):
    return pl.pallas_call(
        sum_kernel, out_shape=shape((copies, T + TAIL, T), bf16), in_specs=[VMEM], out_specs=VMEM, compiler_params=params(16), name=name
    )(packed)


def roots_call(owners, block_layer, damping, packed, grads, prev):
    return pl.pallas_call(
        main_kernel,
        out_shape=[shape((NB, B, B), f32), shape((8, 8, T), f32), shape((8, T), f32)],
        in_specs=[ANY, ANY, ANY, VMEM, VMEM, VMEM],
        out_specs=[VMEM, VMEM, VMEM],
        scratch_shapes=[
            pltpu.SMEM((NB, 2), jnp.int32),
            pltpu.SMEM((NB,), jnp.int32),
            pltpu.SMEM((LAYERS,), f32),
            pltpu.SemaphoreType.DMA((3,)),
            pltpu.VMEM((B, B), f32),
            pltpu.VMEM((2, 3, B, B), f32),
            pltpu.VMEM((2, 3, B, B), bf16),
            pltpu.VMEM((2, B, B), f32),
            pltpu.VMEM((2, B, B), bf16),
            pltpu.VMEM((2, B, B), f32),
            pltpu.VMEM((2, B, B), bf16),
            pltpu.VMEM((2, B, B), f32),
            pltpu.VMEM((2, B, B), bf16),
            pltpu.VMEM((4, B, B), bf16),
            pltpu.VMEM((2, B, B), f32),
        ],
        compiler_params=params(40),
        name="roots_and_update",
    )(owners, block_layer, damping, packed, grads[0], prev)


def graft_call(hot, sums, update):
    return pl.pallas_call(
        scale_kernel,
        out_shape=shape((1, NB, B, B), bf16),
        in_specs=[VMEM, VMEM, VMEM],
        out_specs=ANY,
        scratch_shapes=[pltpu.VMEM((NB, B, B), bf16), pltpu.SemaphoreType.DMA((NB, PIECES))],
        compiler_params=params(16),
        name="graft",
    )(hot, sums, update)


def per_device(grads, prev_roots, damping, block_layer, owners):
    packed = lax.all_to_all(gram_call(owners, grads), PLANE, 0, 0)
    packed = lax.all_to_all(sum_call(packed, 4, "plane_sum"), "z", 0, 0)
    packed = lax.all_to_all(sum_call(packed, CHUNKS, "line_sum"), PLANE, 0, 0)
    update, sums, hot = roots_call(owners, block_layer, damping, packed, grads, prev_roots.reshape(2 * NB, B, B))
    return graft_call(hot, lax.all_to_all(sums, COLUMN, 0, 0), update)


def solution(mesh):
    dp, mp = ("z", "y", "x"), ("h", "c")
    fine = Mesh(mesh.devices.reshape(4, 4, 4, 4, 2), dp + mp)
    return jax.shard_map(
        per_device,
        mesh=fine,
        in_specs=(P(dp, mp, None, None), P(mp, None, None, None), P(), P(mp), P(mp, None)),
        out_specs=P(dp, mp, None, None),
        check_vma=False,
    )
```

```python
import math

import jax
import jax.numpy as jnp
from jax import lax
from jax.experimental import pallas as pl
from jax.experimental.pallas import tpu as pltpu
from jax.sharding import Mesh, PartitionSpec as P

B = 512
NB = 2
LAYERS = 4
SHARDS = 64
NORM_EPSILON = 1e-06
PLANE = ("y", "x")
COLUMN = ("h", "c")
T = 128
NT = B // T
CHUNKS = 16
ROWS = B // CHUNKS
SPAN = 240.0
HALF = SPAN / 2 * math.log(2.0)
UNIT = 1.0 / (SPAN * math.log(2.0))
PIECES = 2
TAIL = 16
TINY = 1e-30
f32, bf16 = jnp.float32, jnp.bfloat16
VMEM = pl.BlockSpec(memory_space=pltpu.VMEM)
SMEM = pl.BlockSpec(memory_space=pltpu.SMEM)
ANY = pl.BlockSpec(memory_space=pltpu.HBM)


def params(mib):
    return pltpu.CompilerParams(vmem_limit_bytes=mib << 20)


def dot(a, b):
    return jnp.dot(a, b, preferred_element_type=f32)


def refreshed(owners):
    f = [owners[0, 0] >= 0, owners[0, 1] >= 0, owners[1, 0] >= 0, owners[1, 1] >= 0]
    first = jnp.where(f[0], 0, jnp.where(f[1], 1, 2))
    last = jnp.where(f[3], 3, jnp.where(f[2], 2, 1))
    return first, last


def top_of(x):
    top = jnp.max(jnp.max(jnp.abs(x), axis=0, keepdims=True), axis=1, keepdims=True)
    return jnp.maximum(top * 1.008, TINY).astype(bf16).astype(f32)


def encode(x, gain):
    size = jnp.exp2(jnp.minimum(jnp.abs(x) * gain, SPAN) - SPAN / 2)
    return jnp.where(x < 0, -size, size).astype(bf16)


def decode(code, top):
    code = code.astype(f32)
    size = (jnp.log(jnp.abs(code)) + HALF) * top
    return jnp.where(code < 0, -size, size)


def parts3(x):
    hi = x.astype(bf16).astype(f32)
    mid = (x - hi).astype(bf16).astype(f32)
    return [hi, mid, x - hi - mid]


def tail_of(diags, tops):
    rows = parts3(diags[0]) + parts3(diags[1]) + [jnp.broadcast_to(t, (1, T)) for t in tops]
    return jnp.concatenate(rows + [jnp.zeros((8, T), f32)], axis=0).astype(bf16)


def read_tail(tail):
    t = tail.astype(f32)
    return [t[0:1] + t[1:2] + t[2:3], t[3:4] + t[4:5] + t[5:6]], [t[6:7] * UNIT, t[7:8] * UNIT]


def kind(k, j):
    if k * ROWS > j * T + T - 1:
        return 1
    return -1 if k * ROWS + ROWS - 1 < j * T else 0


def gram_kernel(owners_hbm, g_hbm, out, owners, g, grams, flip, sems):
    copies = [pltpu.make_async_copy(owners_hbm, owners, sems.at[NB])]
    copies += [pltpu.make_async_copy(g_hbm.at[0, b], g.at[b], sems.at[b]) for b in range(NB)]
    for c in copies:
        c.start()
    for c in copies:
        c.wait()
    for slot, stat in enumerate(refreshed(owners)):
        block = g[stat // 2]

        top, bottom = slice(0, B // 2), slice(B // 2, B)
        quarters = [(top, top), (bottom, top) if slot == 0 else (top, bottom), (bottom, bottom)]

        @pl.when(stat % 2 == 0)
        def _():
            for r, c in quarters:
                grams[slot, r, c] = lax.dot_general(block[r], block[c], (((1,), (1,)), ((), ())), preferred_element_type=f32)

        @pl.when(stat % 2 == 1)
        def _():
            flip[...] = block.T
            for r, c in quarters:
                grams[slot, r, c] = dot(flip[r, :], block[:, c])

    row = lax.broadcasted_iota(jnp.int32, (ROWS, T), 0)
    col = lax.broadcasted_iota(jnp.int32, (ROWS, T), 1)
    most = [jnp.zeros((ROWS, T), f32), jnp.zeros((ROWS, T), f32)]
    diag = [[jnp.zeros((1, T), f32) for _ in range(NT)] for _ in range(2)]
    for k in range(CHUNKS):
        rows = slice(k * ROWS, (k + 1) * ROWS)
        for j in range(NT):
            cols = slice(j * T, (j + 1) * T)
            where = kind(k, j)
            if where:
                s = (1 - where) // 2
                most[s] = jnp.maximum(most[s], jnp.abs(grams[s, rows, cols]))
            else:
                gap = row - col + (k * ROWS - j * T)
                for s in range(2):
                    x = grams[s, rows, cols]
                    diag[s][j] = diag[s][j] + jnp.sum(jnp.where(gap == 0, x, 0.0), axis=0, keepdims=True)
                    most[s] = jnp.maximum(most[s], jnp.where(gap > 0 if s == 0 else gap < 0, jnp.abs(x), 0.0))
    tops = [top_of(m) for m in most]
    gains = [SPAN / t for t in tops]
    tails = [tail_of([diag[0][j], diag[1][j]], tops) for j in range(NT)]
    for k in range(CHUNKS):
        rows = slice(k * ROWS, (k + 1) * ROWS)
        for j in range(NT):
            cols = slice(j * T, (j + 1) * T)
            where = kind(k, j)
            if where:
                s = (1 - where) // 2
                code = encode(grams[s, rows, cols], gains[s])
            else:
                lower = row + k * ROWS >= col + j * T
                code = encode(jnp.where(lower, grams[0, rows, cols], grams[1, rows, cols]), jnp.where(lower, gains[0], gains[1]))
            out[k, j * ROWS : (j + 1) * ROWS, :] = code
        out[k, T : T + TAIL, :] = tails[k * ROWS // T]


def chunk_place():
    mine = lax.axis_index("y") * 4 + lax.axis_index("x")
    r = lax.broadcasted_iota(jnp.int32, (T, T), 0)
    return mine * ROWS + r % ROWS, (r // ROWS) * T + lax.broadcasted_iota(jnp.int32, (T, T), 1)


def add_parts(parts, lower):
    total = jnp.zeros((T, T), f32)
    diag = [jnp.zeros((1, T), f32), jnp.zeros((1, T), f32)]
    for p in range(parts.shape[0]):
        d, tops = read_tail(parts[p, T : T + TAIL, :])
        total = total + decode(parts[p, :T, :], jnp.where(lower, tops[0], tops[1]))
        diag = [diag[0] + d[0], diag[1] + d[1]]
    return total, diag


def code_total(total, row, col):
    tops = [top_of(jnp.where(row > col, total, 0.0)), top_of(jnp.where(row < col, total, 0.0))]
    return encode(total, jnp.where(row >= col, SPAN / tops[0], SPAN / tops[1])), tops


def sum_kernel(parts, out):
    row, col = chunk_place()
    total, diag = add_parts(parts, row >= col)
    code, tops = code_total(total, row, col)
    tail = tail_of(diag, tops)
    for k in range(out.shape[0]):
        out[k, :T, :] = code
        out[k, T : T + TAIL, :] = tail


def tile(i, j):
    return slice(i * T, (i + 1) * T), slice(j * T, (j + 1) * T)


class Diag:
    def __init__(self, cols, rows):
        self.cols, self.rows = cols, rows

    def map(self, f):
        return Diag([f(c) for c in self.cols], [f(r) for r in self.rows])


def main_kernel(owners_hbm, layers_hbm, damping_hbm, packed, g, prev, update, sums, hot, owners, layers, damping, sems, c_ref, x_ref, xo, s_ref, so, f_ref, fo, h_ref, ho, roots, accs):
    copies = [
        pltpu.make_async_copy(owners_hbm, owners, sems.at[0]),
        pltpu.make_async_copy(layers_hbm, layers, sems.at[1]),
        pltpu.make_async_copy(damping_hbm, damping, sems.at[2]),
    ]
    for c in copies:
        c.start()
    row = lax.broadcasted_iota(jnp.int32, (T, T), 0)
    col = lax.broadcasted_iota(jnp.int32, (T, T), 1)
    mask = row == col
    lower = row > col
    crow = lax.broadcasted_iota(jnp.int32, (ROWS, T), 0)
    ccol = lax.broadcasted_iota(jnp.int32, (ROWS, T), 1)
    squares = [jnp.zeros((ROWS, T), f32), jnp.zeros((ROWS, T), f32)]
    diags = [[], []]
    for k in range(CHUNKS):
        pieces, tops = read_tail(packed[k, T : T + TAIL, :])
        ta, tb = [t * (1.0 / (SHARDS * B)) for t in tops]
        if k * ROWS % T == 0:
            for s in range(2):
                diags[s].append(pieces[s] * (1.0 / (SHARDS * B)))
        for j in range(NT):
            code = packed[k, j * ROWS : (j + 1) * ROWS, :]
            low, high = k * ROWS - j * T - (T - 1), k * ROWS + ROWS - 1 - j * T
            if low > 0:
                x = decode(code, ta)
                squares[0] = squares[0] + x * x
            elif high < 0:
                x = decode(code, tb)
                squares[1] = squares[1] + x * x
            else:
                r, c = crow + k * ROWS, ccol + j * T
                x = decode(code, jnp.where(r > c, ta, tb))
                x = jnp.where(r == c, 0.0, x)
                q = x * x
                squares[0] = squares[0] + jnp.where(r > c, q, 0.0)
                squares[1] = squares[1] + jnp.where(r > c, 0.0, q)
            c_ref[k * ROWS : (k + 1) * ROWS, j * T : (j + 1) * T] = x

    for c in copies:
        c.wait()
    ids = refreshed(owners)
    for n in range(2 * NB):

        @pl.when((ids[0] != n) & (ids[1] != n))
        def _():
            roots[n] = prev[n]

    def total(v):
        return jnp.sum(jnp.sum(v, axis=0, keepdims=True), axis=1, keepdims=True)

    def column(r):
        return jnp.sum(jnp.where(mask, r, 0.0), axis=1, keepdims=True)

    dx, scales = [None, None], [None, None]
    for s in range(2):
        d = jnp.concatenate(diags[s], axis=0)
        trace = total(d)
        shift = damping[layers[ids[s] // 2]] * trace * (1.0 / B)
        d = d + shift
        z = 2.5 / jnp.sqrt(2.0 * total(squares[s]) + total(d * d))
        scales[s] = jnp.sqrt(jnp.sqrt(z))
        rows = [1.25 - 0.25 * (z * d[i : i + 1, :]) for i in range(NT)]
        dx[s] = Diag([column(r) for r in rows], rows)
        w = -0.25 * z
        for i in range(NT):
            for j in range(i + 1):
                r, c = tile(i, j)
                if i == j:
                    x = c_ref[r, c]
                    x = jnp.where(lower if s == 0 else row < col, x, x.T) * w
                    x_ref[s, 0, r, c] = x
                    xo[s, 0, r, c] = x.astype(bf16)
                else:
                    x = (c_ref[r, c] if s == 0 else c_ref[c, r]) * w
                    a, b = ((r, c), (c, r)) if s == 0 else ((c, r), (r, c))
                    x_ref[s, 0, a[0], a[1]] = x
                    xo[s, 0, a[0], a[1]] = x.astype(bf16)
                    x = x.T
                    x_ref[s, 0, b[0], b[1]] = x
                    xo[s, 0, b[0], b[1]] = x.astype(bf16)

    def finish(acc, off, da, db, keep, diag):
        for j in range(NT):
            for i in range(NT if j >= NT // 2 else NT // 2):
                r, c = tile(i, j)
                base = acc[r, c]
                if i == j:
                    on = jnp.where(mask, base, 0.0)
                    diag.cols.append(jnp.sum(on, axis=1, keepdims=True) + da.cols[i] * db.cols[i])
                    diag.rows.append(jnp.sum(on, axis=0, keepdims=True) + da.rows[i] * db.rows[i])
                    keep(r, c, jnp.where(mask, 0.0, base + off(i, j, r, c)), diag.rows[i])
                else:
                    x = base + off(i, j, r, c)
                    keep(r, c, x, None)
                    if j >= NT // 2 and i < NT // 2:
                        keep(c, r, x.T, None)
                if i % 2:
                    yield

    def product(acc, a, b):
        left, right = slice(0, B // 2), slice(B // 2, B)
        acc[left, left] = dot(a[left, :], b[:, left])
        yield
        acc[left, right] = dot(a[left, :], b[:, right])
        yield
        acc[right, right] = dot(a[right, :], b[:, right])
        yield

    def together(work, rest):
        for _ in work:
            next(rest, None)
            next(rest, None)
        for _ in rest:
            pass

    def square_off(d, ref):
        return lambda i, j, r, c: ref[r, c] * (d.cols[i] + d.rows[j])

    def cross_off(da, aref, db, bref):
        return lambda i, j, r, c: da.cols[i] * bref[r, c] + aref[r, c] * db.rows[j]

    def keep_in(full, off):
        def keep(r, c, x, on):
            full[r, c] = x
            off[r, c] = x.astype(bf16)

        return keep

    def newton(s):
        x = [dx[s]]
        for it in range(2):
            d = x[it]
            ds, df, dn = Diag([], []), Diag([], []), Diag([], [])
            yield product(accs.at[s], xo.at[s, it], xo.at[s, it]), finish(accs.at[s], square_off(d, x_ref.at[s, it]), d, d, keep_in(s_ref.at[s], so.at[s]), ds)
            yield product(accs.at[s], so.at[s], so.at[s]), finish(accs.at[s], square_off(ds, s_ref.at[s]), ds, ds, keep_in(f_ref.at[s], fo.at[s]), df)
            dy = d.map(lambda v: v - 1.25)
            yield (
                product(accs.at[s], fo.at[s], xo.at[s, it]),
                finish(accs.at[s], cross_off(df, f_ref.at[s], dy, x_ref.at[s, it]), df, dy, keep_in(x_ref.at[s, it + 1], xo.at[s, it + 1]), dn),
            )
            x.append(dn.map(lambda v: v + 1.25))
            if it == 0:
                dh = Diag([], [])
                yield (
                    product(accs.at[s], xo.at[s, 0], xo.at[s, 1]),
                    finish(accs.at[s], cross_off(x[0], x_ref.at[s, 0], x[1], x_ref.at[s, 1]), x[0], x[1], keep_in(h_ref.at[s], ho.at[s]), dh),
                )

        def keep(r, c, v, on):
            if on is not None:
                v = jnp.where(mask, on, v)
            roots[ids[s], r, c] = (v * scales[s]).astype(bf16)

        yield (
            product(accs.at[s], ho.at[s], xo.at[s, 2]),
            finish(accs.at[s], cross_off(dh, h_ref.at[s], x[2], x_ref.at[s, 2]), dh, x[2], keep, Diag([], [])),
        )

    chains = [newton(0), newton(1)]
    waiting = None
    for turn in range(16):
        work, rest = next(chains[turn % 2])
        together(work, iter(()) if waiting is None else waiting)
        waiting = rest
    together(iter(()), waiting)
    lane = lax.broadcasted_iota(jnp.int32, (8, T), 1)
    line = lax.broadcasted_iota(jnp.int32, (8, T), 0)
    tail = jnp.zeros((8, T), f32)
    ones = jnp.zeros((8, T), f32)
    for b in range(NB):
        ones = jnp.where((lane == layers[b]) & (line == b), 1.0, ones)
    hot[...] = ones
    for b in range(NB):
        half = dot(roots[2 * b], g[b]).astype(bf16)
        u = dot(half, roots[2 * b + 1])
        update[b] = u
        x = g[b].astype(f32)
        hit = lane == layers[b]
        tail = tail + jnp.where(hit & (line == 0), total(x * x), 0.0) + jnp.where(hit & (line == 1), total(u * u), 0.0)
    for k in range(sums.shape[0]):
        sums[k] = tail


def scale_kernel(hot, sums, update, out, scaled, sems):
    total = sums[0]
    for k in range(1, sums.shape[0]):
        total = total + sums[k]
    ratio = jnp.sqrt((total[0:1] + NORM_EPSILON) / (total[1:2] + NORM_EPSILON))
    copies = []
    for b in range(NB):
        mine = jnp.sum(hot[b : b + 1] * ratio, axis=1, keepdims=True)
        for h in range(PIECES):
            rows = pl.ds(h * (B // PIECES), B // PIECES)
            scaled[b, rows, :] = (update[b, rows, :] * mine).astype(bf16)
            copies.append(pltpu.make_async_copy(scaled.at[b, rows], out.at[0, b, rows], sems.at[b, h]))
            copies[-1].start()
    for c in copies:
        c.wait()


shape = jax.ShapeDtypeStruct


def gram_call(owners, grads):
    return pl.pallas_call(
        gram_kernel,
        out_shape=shape((CHUNKS, T + TAIL, T), bf16),
        in_specs=[ANY, ANY],
        out_specs=VMEM,
        scratch_shapes=[
            pltpu.SMEM((NB, 2), jnp.int32),
            pltpu.VMEM((NB, B, B), bf16),
            pltpu.VMEM((2, B, B), f32),
            pltpu.VMEM((B, B), bf16),
            pltpu.SemaphoreType.DMA((NB + 1,)),
        ],
        compiler_params=params(53),
        name="gram",
    )(owners, grads)


def sum_call(packed, copies, name):
    return pl.pallas_call(
        sum_kernel, out_shape=shape((copies, T + TAIL, T), bf16), in_specs=[VMEM], out_specs=VMEM, compiler_params=params(16), name=name
    )(packed)


def roots_call(owners, block_layer, damping, packed, grads, prev):
    return pl.pallas_call(
        main_kernel,
        out_shape=[shape((NB, B, B), f32), shape((8, 8, T), f32), shape((8, T), f32)],
        in_specs=[ANY, ANY, ANY, VMEM, VMEM, VMEM],
        out_specs=[VMEM, VMEM, VMEM],
        scratch_shapes=[
            pltpu.SMEM((NB, 2), jnp.int32),
            pltpu.SMEM((NB,), jnp.int32),
            pltpu.SMEM((LAYERS,), f32),
            pltpu.SemaphoreType.DMA((3,)),
            pltpu.VMEM((B, B), f32),
            pltpu.VMEM((2, 3, B, B), f32),
            pltpu.VMEM((2, 3, B, B), bf16),
            pltpu.VMEM((2, B, B), f32),
            pltpu.VMEM((2, B, B), bf16),
            pltpu.VMEM((2, B, B), f32),
            pltpu.VMEM((2, B, B), bf16),
            pltpu.VMEM((2, B, B), f32),
            pltpu.VMEM((2, B, B), bf16),
            pltpu.VMEM((4, B, B), bf16),
            pltpu.VMEM((2, B, B), f32),
        ],
        compiler_params=params(40),
        name="roots_and_update",
    )(owners, block_layer, damping, packed, grads[0], prev)


def graft_call(hot, sums, update):
    return pl.pallas_call(
        scale_kernel,
        out_shape=shape((1, NB, B, B), bf16),
        in_specs=[VMEM, VMEM, VMEM],
        out_specs=ANY,
        scratch_shapes=[pltpu.VMEM((NB, B, B), bf16), pltpu.SemaphoreType.DMA((NB, PIECES))],
        compiler_params=params(16),
        name="graft",
    )(hot, sums, update)


def per_device(grads, prev_roots, damping, block_layer, owners):
    packed = lax.all_to_all(gram_call(owners, grads), PLANE, 0, 0)
    packed = lax.all_to_all(sum_call(packed, 4, "plane_sum"), "z", 0, 0)
    packed = lax.all_to_all(sum_call(packed, CHUNKS, "line_sum"), PLANE, 0, 0)
    update, sums, hot = roots_call(owners, block_layer, damping, packed, grads, prev_roots.reshape(2 * NB, B, B))
    return graft_call(hot, lax.all_to_all(sums, COLUMN, 0, 0), update)


def solution(mesh):
    dp, mp = ("z", "y", "x"), ("h", "c")
    fine = Mesh(mesh.devices.reshape(4, 4, 4, 4, 2), dp + mp)
    return jax.shard_map(
        per_device,
        mesh=fine,
        in_specs=(P(dp, mp, None, None), P(mp, None, None, None), P(), P(mp), P(mp, None)),
        out_specs=P(dp, mp, None, None),
        check_vma=False,
    )
```

```python
import math

import jax
import jax.numpy as jnp
from jax import lax
from jax.experimental import pallas as pl
from jax.experimental.pallas import tpu as pltpu
from jax.sharding import Mesh, PartitionSpec as P

B = 512
NB = 2
LAYERS = 4
SHARDS = 64
NORM_EPSILON = 1e-06
PLANE = ("y", "x")
COLUMN = ("h", "c")
T = 128
NT = B // T
CHUNKS = 16
ROWS = B // CHUNKS
SPAN = 240.0
HALF = SPAN / 2 * math.log(2.0)
UNIT = 1.0 / (SPAN * math.log(2.0))
PIECES = 2
TAIL = 16
TINY = 1e-30
f32, bf16 = jnp.float32, jnp.bfloat16
VMEM = pl.BlockSpec(memory_space=pltpu.VMEM)
SMEM = pl.BlockSpec(memory_space=pltpu.SMEM)
ANY = pl.BlockSpec(memory_space=pltpu.HBM)


def params(mib):
    return pltpu.CompilerParams(vmem_limit_bytes=mib << 20)


def dot(a, b):
    return jnp.dot(a, b, preferred_element_type=f32)


def refreshed(owners):
    f = [owners[0, 0] >= 0, owners[0, 1] >= 0, owners[1, 0] >= 0, owners[1, 1] >= 0]
    first = jnp.where(f[0], 0, jnp.where(f[1], 1, 2))
    last = jnp.where(f[3], 3, jnp.where(f[2], 2, 1))
    return first, last


def top_of(x):
    top = jnp.max(jnp.max(jnp.abs(x), axis=0, keepdims=True), axis=1, keepdims=True)
    return jnp.maximum(top * 1.008, TINY).astype(bf16).astype(f32)


def encode(x, gain):
    size = jnp.exp2(jnp.minimum(jnp.abs(x) * gain, SPAN) - SPAN / 2)
    return jnp.where(x < 0, -size, size).astype(bf16)


def decode(code, top):
    code = code.astype(f32)
    size = (jnp.log(jnp.abs(code)) + HALF) * top
    return jnp.where(code < 0, -size, size)


def parts3(x):
    hi = x.astype(bf16).astype(f32)
    mid = (x - hi).astype(bf16).astype(f32)
    return [hi, mid, x - hi - mid]


def tail_of(diags, tops):
    rows = parts3(diags[0]) + parts3(diags[1]) + [jnp.broadcast_to(t, (1, T)) for t in tops]
    return jnp.concatenate(rows + [jnp.zeros((8, T), f32)], axis=0).astype(bf16)


def read_tail(tail):
    t = tail.astype(f32)
    return [t[0:1] + t[1:2] + t[2:3], t[3:4] + t[4:5] + t[5:6]], [t[6:7] * UNIT, t[7:8] * UNIT]


def kind(k, j):
    if k * ROWS > j * T + T - 1:
        return 1
    return -1 if k * ROWS + ROWS - 1 < j * T else 0


def gram_kernel(owners_hbm, g_hbm, out, owners, g, grams, flip, sems):
    copies = [pltpu.make_async_copy(owners_hbm, owners, sems.at[NB])]
    copies += [pltpu.make_async_copy(g_hbm.at[0, b], g.at[b], sems.at[b]) for b in range(NB)]
    for c in copies:
        c.start()
    for c in copies:
        c.wait()
    for slot, stat in enumerate(refreshed(owners)):
        block = g[stat // 2]

        top, bottom = slice(0, B // 2), slice(B // 2, B)
        quarters = [(top, top), (bottom, top) if slot == 0 else (top, bottom), (bottom, bottom)]

        @pl.when(stat % 2 == 0)
        def _():
            for r, c in quarters:
                grams[slot, r, c] = lax.dot_general(block[r], block[c], (((1,), (1,)), ((), ())), preferred_element_type=f32)

        @pl.when(stat % 2 == 1)
        def _():
            flip[...] = block.T
            for r, c in quarters:
                grams[slot, r, c] = dot(flip[r, :], block[:, c])

    row = lax.broadcasted_iota(jnp.int32, (ROWS, T), 0)
    col = lax.broadcasted_iota(jnp.int32, (ROWS, T), 1)
    most = [jnp.zeros((ROWS, T), f32), jnp.zeros((ROWS, T), f32)]
    diag = [[jnp.zeros((1, T), f32) for _ in range(NT)] for _ in range(2)]
    for k in range(CHUNKS):
        rows = slice(k * ROWS, (k + 1) * ROWS)
        for j in range(NT):
            cols = slice(j * T, (j + 1) * T)
            where = kind(k, j)
            if where:
                s = (1 - where) // 2
                most[s] = jnp.maximum(most[s], jnp.abs(grams[s, rows, cols]))
            else:
                gap = row - col + (k * ROWS - j * T)
                for s in range(2):
                    x = grams[s, rows, cols]
                    diag[s][j] = diag[s][j] + jnp.sum(jnp.where(gap == 0, x, 0.0), axis=0, keepdims=True)
                    most[s] = jnp.maximum(most[s], jnp.where(gap > 0 if s == 0 else gap < 0, jnp.abs(x), 0.0))
    tops = [top_of(m) for m in most]
    gains = [SPAN / t for t in tops]
    tails = [tail_of([diag[0][j], diag[1][j]], tops) for j in range(NT)]
    for k in range(CHUNKS):
        rows = slice(k * ROWS, (k + 1) * ROWS)
        for j in range(NT):
            cols = slice(j * T, (j + 1) * T)
            where = kind(k, j)
            if where:
                s = (1 - where) // 2
                code = encode(grams[s, rows, cols], gains[s])
            else:
                lower = row + k * ROWS >= col + j * T
                code = encode(jnp.where(lower, grams[0, rows, cols], grams[1, rows, cols]), jnp.where(lower, gains[0], gains[1]))
            out[k, j * ROWS : (j + 1) * ROWS, :] = code
        out[k, T : T + TAIL, :] = tails[k * ROWS // T]


def chunk_place():
    mine = lax.axis_index("y") * 4 + lax.axis_index("x")
    r = lax.broadcasted_iota(jnp.int32, (T, T), 0)
    return mine * ROWS + r % ROWS, (r // ROWS) * T + lax.broadcasted_iota(jnp.int32, (T, T), 1)


def add_parts(parts, lower):
    diag = [jnp.zeros((1, T), f32), jnp.zeros((1, T), f32)]
    scales = []
    for p in range(parts.shape[0]):
        d, tops = read_tail(parts[p, T : T + TAIL, :])
        scales.append(tops)
        diag = [diag[0] + d[0], diag[1] + d[1]]
    blocks = []
    for h in range(NT):
        rows = slice(h * ROWS, (h + 1) * ROWS)
        total = jnp.zeros((ROWS, T), f32)
        for p in range(parts.shape[0]):
            total = total + decode(parts[p, rows, :], jnp.where(lower[rows], scales[p][0], scales[p][1]))
        blocks.append(total)
    return jnp.concatenate(blocks, axis=0), diag


def code_total(total, row, col):
    tops = [top_of(jnp.where(row > col, total, 0.0)), top_of(jnp.where(row < col, total, 0.0))]
    return encode(total, jnp.where(row >= col, SPAN / tops[0], SPAN / tops[1])), tops


def sum_kernel(parts, out):
    row, col = chunk_place()
    total, diag = add_parts(parts, row >= col)
    code, tops = code_total(total, row, col)
    tail = tail_of(diag, tops)
    for k in range(out.shape[0]):
        out[k, :T, :] = code
        out[k, T : T + TAIL, :] = tail


def tile(i, j):
    return slice(i * T, (i + 1) * T), slice(j * T, (j + 1) * T)


class Diag:
    def __init__(self, cols, rows):
        self.cols, self.rows = cols, rows

    def map(self, f):
        return Diag([f(c) for c in self.cols], [f(r) for r in self.rows])


def main_kernel(owners_hbm, layers_hbm, damping_hbm, packed, g, prev, update, sums, hot, owners, layers, damping, sems, c_ref, x_ref, xo, s_ref, so, f_ref, fo, h_ref, ho, roots, accs):
    copies = [
        pltpu.make_async_copy(owners_hbm, owners, sems.at[0]),
        pltpu.make_async_copy(layers_hbm, layers, sems.at[1]),
        pltpu.make_async_copy(damping_hbm, damping, sems.at[2]),
    ]
    for c in copies:
        c.start()
    row = lax.broadcasted_iota(jnp.int32, (T, T), 0)
    col = lax.broadcasted_iota(jnp.int32, (T, T), 1)
    mask = row == col
    lower = row > col
    crow = lax.broadcasted_iota(jnp.int32, (ROWS, T), 0)
    ccol = lax.broadcasted_iota(jnp.int32, (ROWS, T), 1)
    squares = [jnp.zeros((ROWS, T), f32), jnp.zeros((ROWS, T), f32)]
    diags = [[], []]
    for k in range(CHUNKS):
        pieces, tops = read_tail(packed[k, T : T + TAIL, :])
        ta, tb = [t * (1.0 / (SHARDS * B)) for t in tops]
        if k * ROWS % T == 0:
            for s in range(2):
                diags[s].append(pieces[s] * (1.0 / (SHARDS * B)))
        for j in range(NT):
            code = packed[k, j * ROWS : (j + 1) * ROWS, :]
            low, high = k * ROWS - j * T - (T - 1), k * ROWS + ROWS - 1 - j * T
            if low > 0:
                x = decode(code, ta)
                squares[0] = squares[0] + x * x
            elif high < 0:
                x = decode(code, tb)
                squares[1] = squares[1] + x * x
            else:
                r, c = crow + k * ROWS, ccol + j * T
                x = decode(code, jnp.where(r > c, ta, tb))
                x = jnp.where(r == c, 0.0, x)
                q = x * x
                squares[0] = squares[0] + jnp.where(r > c, q, 0.0)
                squares[1] = squares[1] + jnp.where(r > c, 0.0, q)
            c_ref[k * ROWS : (k + 1) * ROWS, j * T : (j + 1) * T] = x

    for c in copies:
        c.wait()
    ids = refreshed(owners)
    for n in range(2 * NB):

        @pl.when((ids[0] != n) & (ids[1] != n))
        def _():
            roots[n] = prev[n]

    def total(v):
        return jnp.sum(jnp.sum(v, axis=0, keepdims=True), axis=1, keepdims=True)

    def column(r):
        return jnp.sum(jnp.where(mask, r, 0.0), axis=1, keepdims=True)

    dx, scales = [None, None], [None, None]
    for s in range(2):
        d = jnp.concatenate(diags[s], axis=0)
        trace = total(d)
        shift = damping[layers[ids[s] // 2]] * trace * (1.0 / B)
        d = d + shift
        z = 2.5 / jnp.sqrt(2.0 * total(squares[s]) + total(d * d))
        scales[s] = jnp.sqrt(jnp.sqrt(z))
        rows = [1.25 - 0.25 * (z * d[i : i + 1, :]) for i in range(NT)]
        dx[s] = Diag([column(r) for r in rows], rows)
        w = -0.25 * z
        for i in range(NT):
            for j in range(i + 1):
                r, c = tile(i, j)
                if i == j:
                    x = c_ref[r, c]
                    x = jnp.where(lower if s == 0 else row < col, x, x.T) * w
                    x_ref[s, 0, r, c] = x
                    xo[s, 0, r, c] = x.astype(bf16)
                else:
                    x = (c_ref[r, c] if s == 0 else c_ref[c, r]) * w
                    a, b = ((r, c), (c, r)) if s == 0 else ((c, r), (r, c))
                    x_ref[s, 0, a[0], a[1]] = x
                    xo[s, 0, a[0], a[1]] = x.astype(bf16)
                    x = x.T
                    x_ref[s, 0, b[0], b[1]] = x
                    xo[s, 0, b[0], b[1]] = x.astype(bf16)

    def finish(acc, off, da, db, keep, diag):
        for j in range(NT):
            for i in range(NT if j >= NT // 2 else NT // 2):
                r, c = tile(i, j)
                base = acc[r, c]
                if i == j:
                    on = jnp.where(mask, base, 0.0)
                    diag.cols.append(jnp.sum(on, axis=1, keepdims=True) + da.cols[i] * db.cols[i])
                    diag.rows.append(jnp.sum(on, axis=0, keepdims=True) + da.rows[i] * db.rows[i])
                    keep(r, c, jnp.where(mask, 0.0, base + off(i, j, r, c)), diag.rows[i])
                else:
                    x = base + off(i, j, r, c)
                    keep(r, c, x, None)
                    if j >= NT // 2 and i < NT // 2:
                        keep(c, r, x.T, None)
                if i % 2:
                    yield

    def product(acc, a, b):
        left, right = slice(0, B // 2), slice(B // 2, B)
        acc[left, left] = dot(a[left, :], b[:, left])
        yield
        acc[left, right] = dot(a[left, :], b[:, right])
        yield
        acc[right, right] = dot(a[right, :], b[:, right])
        yield

    def together(work, rest):
        for _ in work:
            next(rest, None)
            next(rest, None)
        for _ in rest:
            pass

    def square_off(d, ref):
        return lambda i, j, r, c: ref[r, c] * (d.cols[i] + d.rows[j])

    def cross_off(da, aref, db, bref):
        return lambda i, j, r, c: da.cols[i] * bref[r, c] + aref[r, c] * db.rows[j]

    def keep_in(full, off):
        def keep(r, c, x, on):
            full[r, c] = x
            off[r, c] = x.astype(bf16)

        return keep

    def newton(s):
        x = [dx[s]]
        for it in range(2):
            d = x[it]
            ds, df, dn = Diag([], []), Diag([], []), Diag([], [])
            yield product(accs.at[s], xo.at[s, it], xo.at[s, it]), finish(accs.at[s], square_off(d, x_ref.at[s, it]), d, d, keep_in(s_ref.at[s], so.at[s]), ds)
            yield product(accs.at[s], so.at[s], so.at[s]), finish(accs.at[s], square_off(ds, s_ref.at[s]), ds, ds, keep_in(f_ref.at[s], fo.at[s]), df)
            dy = d.map(lambda v: v - 1.25)
            yield (
                product(accs.at[s], fo.at[s], xo.at[s, it]),
                finish(accs.at[s], cross_off(df, f_ref.at[s], dy, x_ref.at[s, it]), df, dy, keep_in(x_ref.at[s, it + 1], xo.at[s, it + 1]), dn),
            )
            x.append(dn.map(lambda v: v + 1.25))
            if it == 0:
                dh = Diag([], [])
                yield (
                    product(accs.at[s], xo.at[s, 0], xo.at[s, 1]),
                    finish(accs.at[s], cross_off(x[0], x_ref.at[s, 0], x[1], x_ref.at[s, 1]), x[0], x[1], keep_in(h_ref.at[s], ho.at[s]), dh),
                )

        def keep(r, c, v, on):
            if on is not None:
                v = jnp.where(mask, on, v)
            roots[ids[s], r, c] = (v * scales[s]).astype(bf16)

        yield (
            product(accs.at[s], ho.at[s], xo.at[s, 2]),
            finish(accs.at[s], cross_off(dh, h_ref.at[s], x[2], x_ref.at[s, 2]), dh, x[2], keep, Diag([], [])),
        )

    chains = [newton(0), newton(1)]
    waiting = None
    for turn in range(16):
        work, rest = next(chains[turn % 2])
        together(work, iter(()) if waiting is None else waiting)
        waiting = rest
    together(iter(()), waiting)
    lane = lax.broadcasted_iota(jnp.int32, (8, T), 1)
    line = lax.broadcasted_iota(jnp.int32, (8, T), 0)
    tail = jnp.zeros((8, T), f32)
    ones = jnp.zeros((8, T), f32)
    for b in range(NB):
        ones = jnp.where((lane == layers[b]) & (line == b), 1.0, ones)
    hot[...] = ones
    for b in range(NB):
        half = dot(roots[2 * b], g[b]).astype(bf16)
        u = dot(half, roots[2 * b + 1])
        update[b] = u
        x = g[b].astype(f32)
        hit = lane == layers[b]
        tail = tail + jnp.where(hit & (line == 0), total(x * x), 0.0) + jnp.where(hit & (line == 1), total(u * u), 0.0)
    for k in range(sums.shape[0]):
        sums[k] = tail


def scale_kernel(hot, sums, update, out, scaled, sems):
    total = sums[0]
    for k in range(1, sums.shape[0]):
        total = total + sums[k]
    ratio = jnp.sqrt((total[0:1] + NORM_EPSILON) / (total[1:2] + NORM_EPSILON))
    copies = []
    for b in range(NB):
        mine = jnp.sum(hot[b : b + 1] * ratio, axis=1, keepdims=True)
        for h in range(PIECES):
            rows = pl.ds(h * (B // PIECES), B // PIECES)
            scaled[b, rows, :] = (update[b, rows, :] * mine).astype(bf16)
            copies.append(pltpu.make_async_copy(scaled.at[b, rows], out.at[0, b, rows], sems.at[b, h]))
            copies[-1].start()
    for c in copies:
        c.wait()


shape = jax.ShapeDtypeStruct


def gram_call(owners, grads):
    return pl.pallas_call(
        gram_kernel,
        out_shape=shape((CHUNKS, T + TAIL, T), bf16),
        in_specs=[ANY, ANY],
        out_specs=VMEM,
        scratch_shapes=[
            pltpu.SMEM((NB, 2), jnp.int32),
            pltpu.VMEM((NB, B, B), bf16),
            pltpu.VMEM((2, B, B), f32),
            pltpu.VMEM((B, B), bf16),
            pltpu.SemaphoreType.DMA((NB + 1,)),
        ],
        compiler_params=params(53),
        name="gram",
    )(owners, grads)


def sum_call(packed, copies, name):
    return pl.pallas_call(
        sum_kernel, out_shape=shape((copies, T + TAIL, T), bf16), in_specs=[VMEM], out_specs=VMEM, compiler_params=params(16), name=name
    )(packed)


def roots_call(owners, block_layer, damping, packed, grads, prev):
    return pl.pallas_call(
        main_kernel,
        out_shape=[shape((NB, B, B), f32), shape((8, 8, T), f32), shape((8, T), f32)],
        in_specs=[ANY, ANY, ANY, VMEM, VMEM, VMEM],
        out_specs=[VMEM, VMEM, VMEM],
        scratch_shapes=[
            pltpu.SMEM((NB, 2), jnp.int32),
            pltpu.SMEM((NB,), jnp.int32),
            pltpu.SMEM((LAYERS,), f32),
            pltpu.SemaphoreType.DMA((3,)),
            pltpu.VMEM((B, B), f32),
            pltpu.VMEM((2, 3, B, B), f32),
            pltpu.VMEM((2, 3, B, B), bf16),
            pltpu.VMEM((2, B, B), f32),
            pltpu.VMEM((2, B, B), bf16),
            pltpu.VMEM((2, B, B), f32),
            pltpu.VMEM((2, B, B), bf16),
            pltpu.VMEM((2, B, B), f32),
            pltpu.VMEM((2, B, B), bf16),
            pltpu.VMEM((4, B, B), bf16),
            pltpu.VMEM((2, B, B), f32),
        ],
        compiler_params=params(40),
        name="roots_and_update",
    )(owners, block_layer, damping, packed, grads[0], prev)


def graft_call(hot, sums, update):
    return pl.pallas_call(
        scale_kernel,
        out_shape=shape((1, NB, B, B), bf16),
        in_specs=[VMEM, VMEM, VMEM],
        out_specs=ANY,
        scratch_shapes=[pltpu.VMEM((NB, B, B), bf16), pltpu.SemaphoreType.DMA((NB, PIECES))],
        compiler_params=params(16),
        name="graft",
    )(hot, sums, update)


def per_device(grads, prev_roots, damping, block_layer, owners):
    packed = lax.all_to_all(gram_call(owners, grads), PLANE, 0, 0)
    packed = lax.all_to_all(sum_call(packed, 4, "plane_sum"), "z", 0, 0)
    packed = lax.all_to_all(sum_call(packed, CHUNKS, "line_sum"), PLANE, 0, 0)
    update, sums, hot = roots_call(owners, block_layer, damping, packed, grads, prev_roots.reshape(2 * NB, B, B))
    return graft_call(hot, lax.all_to_all(sums, COLUMN, 0, 0), update)


def solution(mesh):
    dp, mp = ("z", "y", "x"), ("h", "c")
    fine = Mesh(mesh.devices.reshape(4, 4, 4, 4, 2), dp + mp)
    return jax.shard_map(
        per_device,
        mesh=fine,
        in_specs=(P(dp, mp, None, None), P(mp, None, None, None), P(), P(mp), P(mp, None)),
        out_specs=P(dp, mp, None, None),
        check_vma=False,
    )
```
